128 devices in a mesh: fsdp: 8 (over y, x_lo), tp: 16 (over z, x_hi, core).
Axes of the slice: x: 4 (x_hi: 2, x_lo: 2; x = x_hi * 2 + x_lo), y: 4, z: 4, core: 2. Of those that a mesh axis runs over, the one named last changes fastest.
Arguments:
- activ: bfloat16 [2048, 8192], P('tp', 'fsdp'), may hold values from -6 to 6
- policy_gate: bfloat16 [8192, 14336], P(('fsdp', 'tp')), may hold values from -0.0625 to 0.0625
- policy_up: bfloat16 [8192, 14336], P(('fsdp', 'tp')), may hold values from -0.0625 to 0.0625
- policy_down: bfloat16 [14336, 8192], P(None, ('fsdp', 'tp')), may hold values from -0.046875 to 0.046875
- old_gate: bfloat16 [8192, 14336], P(('fsdp', 'tp')), may hold values from -0.0625 to 0.0625
- old_up: bfloat16 [8192, 14336], P(('fsdp', 'tp')), may hold values from -0.0625 to 0.0625
- old_down: bfloat16 [14336, 8192], P(None, ('fsdp', 'tp')), may hold values from -0.046875 to 0.046875
Outputs:
- ffn_out: bfloat16 [2048, 8192], P('tp', 'fsdp')
The draws below stay inside these ranges and needn't reach their ends.
All inputs are finite; a program needn't handle non-finite values.
Results may differ from the reference program's by a relative error of at most 0.03.
Values may be sent and summed in bfloat16 or wider, within the bound.
A program may use at most 128 MiB of HBM per device.

```python
import jax
import jax.numpy as jnp
from jax import lax

D = 8192
FFW = 14336
TOKENS = 2048
N_FSDP = 8


def block_levels(stream_key, dims, shards, low, top_value):
    loudness, own = 1.0, jax.random.fold_in(stream_key, 6)
    for position, shards_of in shards:
        steps = jnp.exp(jax.random.uniform(jax.random.fold_in(own, position), (shards_of,), jnp.float32, low / len(shards), top_value / len(shards)))
        loudness = loudness * jnp.repeat(steps, dims[position] // shards_of).reshape([-1 if axis == position else 1 for axis in range(len(dims))])
    return loudness


def normal_values(rng, shape, deviation, limit, cuts=(), held_as=jnp.bfloat16):
    drawn = deviation * jax.random.normal(rng, shape, jnp.float32)
    if cuts:
        drawn = drawn * block_levels(rng, shape, cuts, -0.22, 0.18)
    return jnp.clip(drawn, -limit, limit).astype(held_as)


def setup_inputs(seed: int = 0) -> dict:
    arg_keys = jax.random.split(jax.random.key(seed), 8)
    return {
        "activ": normal_values(arg_keys[0], (TOKENS, D), 1.0, 6.0, ((0, 16), (1, 8))),
        "policy_gate": normal_values(arg_keys[1], (D, FFW), D ** -0.5, 0.0625, ((0, 128),)),
        "policy_up": normal_values(arg_keys[2], (D, FFW), D ** -0.5, 0.0625, ((0, 128),)),
        "policy_down": normal_values(arg_keys[3], (FFW, D), FFW ** -0.5, 0.046875, ((1, 128),)),
        "old_gate": normal_values(arg_keys[4], (D, FFW), D ** -0.5, 0.0625, ((0, 128),)),
        "old_up": normal_values(arg_keys[5], (D, FFW), D ** -0.5, 0.0625, ((0, 128),)),
        "old_down": normal_values(arg_keys[6], (FFW, D), FFW ** -0.5, 0.046875, ((1, 128),)),
    }


def blend(policy, older):
    return (0.6 * policy.astype(jnp.float32) + 0.4 * older.astype(jnp.float32)).astype(jnp.bfloat16)


def reference(activ, policy_gate, policy_up, policy_down, old_gate, old_up, old_down):
    mixed_gate = blend(policy_gate, old_gate)
    mixed_up = blend(policy_up, old_up)
    mixed_down = blend(policy_down, old_down)
    width_block = D // N_FSDP
    gate = jnp.zeros((TOKENS, FFW), jnp.float32)
    up = jnp.zeros((TOKENS, FFW), jnp.float32)
    for block in range(N_FSDP):
        lower = block * width_block
        inputs = activ[:, lower:lower + width_block]
        gate_block = jnp.dot(inputs, mixed_gate[lower:lower + width_block], preferred_element_type=jnp.float32).astype(jnp.bfloat16)
        up_block = jnp.dot(inputs, mixed_up[lower:lower + width_block], preferred_element_type=jnp.float32).astype(jnp.bfloat16)
        gate_block, up_block = lax.optimization_barrier((gate_block, up_block))
        gate = gate + gate_block.astype(jnp.float32)
        up = up + up_block.astype(jnp.float32)
    hidden = (jax.nn.silu(gate) * up).astype(jnp.bfloat16)
    return jnp.dot(hidden, mixed_down, preferred_element_type=jnp.float32).astype(jnp.bfloat16)
```

```python
import functools

import jax
import jax.numpy as jnp
from jax import lax
from jax.experimental import pallas as pl
from jax.experimental.pallas import tpu as pltpu
from jax.sharding import PartitionSpec as P

MESH = pl.DeviceIdType.MESH
F32, BF16 = jnp.float32, jnp.bfloat16

SIDE = 4
CHIPS = 16
ROWS = 64
UNITS = 896
PLANE = 2048
TOKENS = 2048
QUARTER = 512
BLOCK = 128
FEATS = 1024
CHUNKS = ((0, 256), (256, 256), (512, 384))


def device(x, y, z, c):
    return (y * 2 + x % 2, z * 4 + (x // 2) * 2 + c)


def shift(v, d):
    return lax.rem(v + d, SIDE)


def wait_bytes(ref, sem):
    pltpu.make_async_copy(ref, ref, sem).wait()


def mixed(a, b):
    return (0.6 * a.astype(F32) + 0.4 * b.astype(F32)).astype(BF16)


def kernel(
    act_in, pg_in, pu_in, pd_in, og_in, ou_in, od_in, out,
    mix, old, act, wbuf, dbuf, part, rs, xs, xr, hid, ob, o1, o2s, o2,
    ld, act_ss, act_rs, act_fs, w_ss, w_rs, d_ss, d_rs, d_fs,
    r_ss, r_rs, x_ss, x_rs, h_ss, h_rs, o1_ss, o1_rs, o2_ss, o2_rs,
):
    f, t = lax.axis_index("fsdp"), lax.axis_index("tp")
    y, x_lo = f // 2, lax.rem(f, 2)
    z, x_hi, c = t // 4, lax.rem(t // 2, 2), lax.rem(t, 2)
    x = x_hi * 2 + x_lo
    first = c == 0
    chip = z * SIDE + x
    sibling = device(x, y, z, 1 - c)

    def send(src, dst, send_sem, recv_sem, to):
        pltpu.make_async_remote_copy(
            src_ref=src, dst_ref=dst, send_sem=send_sem, recv_sem=recv_sem, device_id=to, device_id_type=MESH
        ).start()

    def act_block(xx, zz, cc):
        tok = (zz * 4 + (xx // 2) * 2 + cc) * BLOCK
        return act.at[pl.ds(pl.multiple_of(tok, BLOCK), BLOCK), pl.ds(pl.multiple_of(lax.rem(xx, 2) * FEATS, FEATS), FEATS)]

    def weight_rows(xx, zz, cc):
        row = lax.rem(xx, 2) * FEATS + (zz * 2 + xx // 2) * 128 + cc * ROWS
        return pl.ds(pl.multiple_of(row, ROWS), ROWS)

    loads = [
        pltpu.make_async_copy(a, b, ld.at[i])
        for i, (a, b) in enumerate(
            [
                (act_in, act_block(x, z, c)),
                (pg_in, mix.at[0]), (og_in, old.at[0]),
                (pu_in, mix.at[1]), (ou_in, old.at[1]),
                (pd_in, mix.at[2]), (od_in, old.at[2]),
            ]
        )
    ]
    for copy in loads:
        copy.start()

    barrier = pltpu.get_barrier_semaphore()

    def greet(i, carry):
        to = device(shift(x, lax.rem(i // 2, 4)), y, shift(z, i // 8), lax.rem(c + i, 2))
        pl.semaphore_signal(barrier, inc=1, device_id=to, device_id_type=MESH)
        return carry

    lax.fori_loop(1, 32, greet, 0)
    for d in (1, 2, 3):
        pl.semaphore_signal(barrier, inc=1, device_id=device(x, shift(y, d), z, c), device_id_type=MESH)
    pl.semaphore_wait(barrier, 34)

    def along_a(d):
        return jnp.where(first, shift(x, d), x), jnp.where(first, z, shift(z, d))

    def along_b(d):
        return jnp.where(first, x, shift(x, d)), jnp.where(first, shift(z, d), z)

    def block_of(da, db):
        return jnp.where(first, shift(x, da), shift(x, db)), jnp.where(first, shift(z, db), shift(z, da))

    def send_block(xx, zz, to_x, to_z):
        ref = act_block(xx, zz, c)
        send(ref, ref, act_ss, act_rs.at[zz * SIDE + xx], device(to_x, y, to_z, c))

    def share_block(xx, zz):
        ref = act_block(xx, zz, c)
        send(ref, ref, act_ss, act_fs, sibling)

    loads[0].wait()
    for d in (1, 3, 2):
        send_block(x, z, *along_a(d))
    share_block(x, z)

    def send_weights(k):
        c0, cw = CHUNKS[k]
        target = wbuf.at[weight_rows(x, z, c), pl.ds(c0, cw)]

        def blend(p):
            cols = pl.ds(pl.multiple_of(p * UNITS + c0, 128), cw)
            for m in (0, 1):
                mix[m, :, cols] = mixed(mix[m, :, cols], old[m, :, cols])
            return cols

        own = blend(chip)
        pltpu.make_async_copy(mix.at[c, :, own], target, w_rs.at[k]).start()
        send(mix.at[1 - c, :, own], target, w_ss.at[k], w_rs.at[k], sibling)

        def one(i, carry):
            xx, zz = shift(x, lax.rem(i, 4)), shift(z, i // 4)
            cols = blend(zz * SIDE + xx)
            for m in (0, 1):
                send(mix.at[m, :, cols], target, w_ss.at[k], w_rs.at[k], device(xx, y, zz, m))
            return carry

        lax.fori_loop(1, CHIPS, one, 0)

    for copy in loads[1:5]:
        copy.wait()
    send_weights(0)

    for d in (1, 2, 3):
        send_block(x, z, *along_b(d))
    for e in (1, 3, 2):
        xx, zz = block_of(e, 0)
        wait_bytes(act_block(xx, zz, c), act_rs.at[zz * SIDE + xx])
        for d in (1, 3, 2):
            send_block(xx, zz, *along_b(d))
        share_block(xx, zz)

    for k in range(1, len(CHUNKS)):
        send_weights(k)

    for copy in loads[5:]:
        copy.wait()

    def blend_down(i, carry):
        cols = pl.ds(pl.multiple_of(i * UNITS, 128), UNITS)
        mix[2, :, cols] = mixed(mix[2, :, cols], old[2, :, cols])
        return carry

    lax.fori_loop(0, CHIPS, blend_down, 0)

    def send_down():
        target = dbuf.at[weight_rows(x, z, c), :]
        cols = pl.ds(pl.multiple_of(chip * UNITS, 128), UNITS)
        pltpu.make_async_copy(mix.at[2, :, cols], target, d_rs.at[chip]).start()

        def one(i, carry):
            xx, zz = shift(x, lax.rem(i, 4)), shift(z, i // 4)
            cols = pl.ds(pl.multiple_of((zz * SIDE + xx) * UNITS, 128), UNITS)
            send(mix.at[2, :, cols], target, d_ss, d_rs.at[chip], device(xx, y, zz, c))
            return carry

        lax.fori_loop(1, CHIPS, one, 0)

    def share_down():
        def one(i, carry):
            xx, zz = shift(x, lax.rem(i, 4)), shift(z, i // 4)
            ref = dbuf.at[weight_rows(xx, zz, c), :]
            wait_bytes(ref, d_rs.at[zz * SIDE + xx])
            send(ref, ref, d_ss, d_fs, sibling)
            return carry

        lax.fori_loop(0, CHIPS, one, 0)

    for db in (1, 3, 2):
        for da in (0, 1, 3, 2):
            xx, zz = block_of(da, db)
            wait_bytes(act_block(xx, zz, c), act_rs.at[zz * SIDE + xx])
            share_block(xx, zz)
    wait_bytes(act.at[pl.ds(0, TOKENS // 2), :], act_fs)

    def multiply(k):
        c0, cw = CHUNKS[k]
        cols = pl.ds(c0, cw)
        wait_bytes(wbuf.at[:, cols], w_rs.at[k])

        def one(i, carry):
            d = lax.rem(i + 1, SIDE)
            q = shift(y, d)
            rows = pl.ds(pl.multiple_of(q * QUARTER, QUARTER), QUARTER)
            part[rows, cols] = jnp.dot(act[rows, :], wbuf[:, cols], preferred_element_type=F32).astype(BF16)

            @pl.when(i < 3)
            def _():
                send(part.at[rows, cols], rs.at[i, :, cols], r_ss, r_rs.at[k, i], device(x, q, z, c))

            return carry

        lax.fori_loop(0, SIDE, one, 0)

    def reduce(k):
        c0, cw = CHUNKS[k]
        cols = pl.ds(c0, cw)
        for i in range(3):
            wait_bytes(rs.at[i, :, cols], r_rs.at[k, i])

        def one(j, carry):
            rows = pl.ds(pl.multiple_of(j * BLOCK, BLOCK), BLOCK)
            total = part[pl.ds(pl.multiple_of(y * QUARTER + j * BLOCK, BLOCK), BLOCK), cols].astype(F32)
            for i in range(3):
                total = total + rs[i, rows, cols].astype(F32)
            xs[rows, cols] = total
            return carry

        lax.fori_loop(0, SIDE, one, 0)
        for j in (0, 1):
            rows = pl.ds(pl.multiple_of((2 * j + 1 - c) * BLOCK, BLOCK), BLOCK)
            send(xs.at[rows, cols], xr.at[pl.ds(j * BLOCK, BLOCK), cols], x_ss, x_rs.at[k], sibling)

    def activate(k):
        c0, cw = CHUNKS[k]
        cols = pl.ds(c0, cw)
        wait_bytes(xr.at[:, cols], x_rs.at[k])
        for j in (0, 1):
            own = xs[pl.ds(pl.multiple_of((2 * j + c) * BLOCK, BLOCK), BLOCK), cols]
            other = xr[pl.ds(j * BLOCK, BLOCK), cols]
            gate, up = jnp.where(first, own, other), jnp.where(first, other, own)
            hid[pl.ds(pl.multiple_of((y * 2 + j) * BLOCK, BLOCK), BLOCK), cols] = (jax.nn.silu(gate) * up).astype(BF16)
        ref = hid.at[pl.ds(pl.multiple_of(y * 2 * BLOCK, 2 * BLOCK), 2 * BLOCK), cols]
        for d in (1, 2, 3):
            send(ref, ref, h_ss, h_rs.at[k, d - 1], device(x, shift(y, d), z, c))

    multiply(0)
    multiply(1)
    reduce(0)
    multiply(2)
    send_down()
    activate(0)
    reduce(1)
    activate(1)
    reduce(2)
    activate(2)
    share_down()
    wait_bytes(dbuf.at[pl.ds(0, PLANE // 2), :], d_fs)
    for k, (c0, cw) in enumerate(CHUNKS):
        for d in (1, 2, 3):
            wait_bytes(hid.at[pl.ds(0, 2 * BLOCK), pl.ds(c0, cw)], h_rs.at[k, d - 1])

    def project(n, carry):
        tile = dbuf[pl.ds(pl.multiple_of(n * 256, 256), 256), :]
        made = lax.dot_general(hid[...], tile, (((1,), (1,)), ((), ())), preferred_element_type=F32).astype(BF16)
        cols = pl.ds(pl.multiple_of(lax.rem(n, 4) * 256, 256), 256)
        for zz in range(SIDE):
            for xh in range(2):
                xx = xh * 2 + n // 4
                a, b = jnp.where(first, zz, xx), jnp.where(first, xx, zz)
                ob[a, b, :, cols] = made[(zz * 2 + xh) * BLOCK : (zz * 2 + xh + 1) * BLOCK]
        return carry

    lax.fori_loop(0, 8, project, 0)
    a, b = jnp.where(first, z, x), jnp.where(first, x, z)
    for d in (1, 2, 3):
        send(ob.at[shift(a, d)], o1.at[d - 1], o1_ss, o1_rs.at[d - 1], device(along_b(d)[0], y, along_b(d)[1], c))
    for i in range(3):
        wait_bytes(o1.at[i], o1_rs.at[i])
    for d in (1, 2, 3, 0):
        bb = shift(b, d)
        total = ob[a, bb].astype(F32)
        for i in range(3):
            total = total + o1[i, bb].astype(F32)
        if d:
            o2s[d - 1] = total.astype(BF16)
            to_x, to_z = along_a(d)
            send(o2s.at[d - 1], o2.at[d - 1], o2_ss, o2_rs.at[d - 1], device(to_x, y, to_z, c))
    for i in range(3):
        wait_bytes(o2.at[i], o2_rs.at[i])
        total = total + o2[i].astype(F32)
    out[...] = total.astype(BF16)

    wait_bytes(act.at[pl.ds(0, 31 * ROWS), :], act_ss)
    for k, (c0, cw) in enumerate(CHUNKS):
        wait_bytes(wbuf.at[pl.ds(0, 31 * ROWS), pl.ds(c0, cw)], w_ss.at[k])
    wait_bytes(dbuf.at[pl.ds(0, 31 * ROWS), :], d_ss)
    wait_bytes(part.at[pl.ds(0, 3 * QUARTER), :], r_ss)
    wait_bytes(xr, x_ss)
    wait_bytes(hid.at[pl.ds(0, 6 * BLOCK), :], h_ss)
    wait_bytes(o1, o1_ss)
    wait_bytes(o2, o2_ss)


def per_device(activ, policy_gate, policy_up, policy_down, old_gate, old_up, old_down):
    sem = pltpu.SemaphoreType.DMA
    n = len(CHUNKS)
    return pl.pallas_call(
        kernel,
        name="layer",
        out_shape=jax.ShapeDtypeStruct((BLOCK, FEATS), BF16),
        in_specs=[pl.BlockSpec(memory_space=pl.ANY)] * 7,
        out_specs=pl.BlockSpec(memory_space=pltpu.VMEM),
        scratch_shapes=[
            pltpu.VMEM((3, ROWS, CHIPS * UNITS), BF16),
            pltpu.VMEM((3, ROWS, CHIPS * UNITS), BF16),
            pltpu.VMEM((TOKENS, PLANE), BF16),
            pltpu.VMEM((PLANE, UNITS), BF16),
            pltpu.VMEM((PLANE, UNITS), BF16),
            pltpu.VMEM((TOKENS, UNITS), BF16),
            pltpu.VMEM((3, QUARTER, UNITS), BF16),
            pltpu.VMEM((QUARTER, UNITS), F32),
            pltpu.VMEM((2 * BLOCK, UNITS), F32),
            pltpu.VMEM((8 * BLOCK, UNITS), BF16),
            pltpu.VMEM((SIDE, SIDE, BLOCK, FEATS), BF16),
            pltpu.VMEM((3, SIDE, BLOCK, FEATS), BF16),
            pltpu.VMEM((3, BLOCK, FEATS), BF16),
            pltpu.VMEM((3, BLOCK, FEATS), BF16),
            sem((7,)),
            sem, sem((CHIPS,)), sem,
            sem((n,)), sem((n,)),
            sem, sem((CHIPS,)), sem,
            sem, sem((n, 3)),
            sem, sem((n,)),
            sem, sem((n, 3)),
            sem, sem((3,)),
            sem, sem((3,)),
        ],
        compiler_params=pltpu.CompilerParams(
            collective_id=0, has_side_effects=True, vmem_limit_bytes=60 << 20
        ),
    )(activ, policy_gate, policy_up, policy_down.T, old_gate, old_up, old_down.T)


def solution(mesh):
    in_specs = (
        P("tp", "fsdp"),
        P(("fsdp", "tp"), None),
        P(("fsdp", "tp"), None),
        P(None, ("fsdp", "tp")),
        P(("fsdp", "tp"), None),
        P(("fsdp", "tp"), None),
        P(None, ("fsdp", "tp")),
    )
    return jax.shard_map(
        per_device, mesh=mesh, in_specs=in_specs, out_specs=P("tp", "fsdp"), check_vma=False
    )
```

```python
import functools

import jax
import jax.numpy as jnp
from jax import lax
from jax.experimental import pallas as pl
from jax.experimental.pallas import tpu as pltpu
from jax.sharding import PartitionSpec as P

MESH = pl.DeviceIdType.MESH
F32, BF16 = jnp.float32, jnp.bfloat16

SIDE = 4
CHIPS = 16
ROWS = 64
UNITS = 896
PLANE = 2048
TOKENS = 2048
QUARTER = 512
HALF = 256
BLOCK = 128
FEATS = 1024
CHUNKS = ((0, 128), (128, 256), (384, 256), (640, 256))


def device(x, y, z, c):
    return (y * 2 + x % 2, z * 4 + (x // 2) * 2 + c)


def shift(v, d):
    return lax.rem(v + d, SIDE)


def wait_bytes(ref, sem):
    pltpu.make_async_copy(ref, ref, sem).wait()


def mixed(a, b):
    return (0.6 * a.astype(F32) + 0.4 * b.astype(F32)).astype(BF16)


def kernel(
    act_in, pg_in, pu_in, pd_in, og_in, ou_in, od_in, out,
    mix, old, act, wbuf, dbuf, part, rl, rf, xs, xr, hid, ob, o1l, o1f, o2s, o2l, o2f,
    ld, act_ss, act_rs, act_fs, w_ss, w_rs, d_ss, d_rs, d_fs,
    r_ss, r_rl, r_rf, x_ss, x_rs, h_ss, h_rs, h_ro, o1_ss, o1_rl, o1_rf, o2_ss, o2_rl, o2_rf,
):
    f, t = lax.axis_index("fsdp"), lax.axis_index("tp")
    y, x_lo = f // 2, lax.rem(f, 2)
    z, x_hi, c = t // 4, lax.rem(t // 2, 2), lax.rem(t, 2)
    x = x_hi * 2 + x_lo
    first = c == 0
    chip = z * SIDE + x
    sibling = device(x, y, z, 1 - c)

    def send(src, dst, send_sem, recv_sem, to):
        pltpu.make_async_remote_copy(
            src_ref=src, dst_ref=dst, send_sem=send_sem, recv_sem=recv_sem, device_id=to, device_id_type=MESH
        ).start()

    def act_block(xx, zz, cc):
        tok = (zz * 4 + (xx // 2) * 2 + cc) * BLOCK
        return act.at[pl.ds(pl.multiple_of(tok, BLOCK), BLOCK), pl.ds(pl.multiple_of(lax.rem(xx, 2) * FEATS, FEATS), FEATS)]

    def weight_rows(xx, zz, cc):
        row = lax.rem(xx, 2) * FEATS + (zz * 2 + xx // 2) * 128 + cc * ROWS
        return pl.ds(pl.multiple_of(row, ROWS), ROWS)

    loads = [
        pltpu.make_async_copy(a, b, ld.at[i])
        for i, (a, b) in enumerate(
            [
                (act_in, act_block(x, z, c)),
                (pg_in, mix.at[0]), (og_in, old.at[0]),
                (pu_in, mix.at[1]), (ou_in, old.at[1]),
                (pd_in, mix.at[2]), (od_in, old.at[2]),
            ]
        )
    ]
    for copy in loads:
        copy.start()

    barrier = pltpu.get_barrier_semaphore()

    def greet(i, carry):
        to = device(shift(x, lax.rem(i // 2, 4)), y, shift(z, i // 8), lax.rem(c + i, 2))
        pl.semaphore_signal(barrier, inc=1, device_id=to, device_id_type=MESH)
        return carry

    lax.fori_loop(1, 32, greet, 0)
    for d in (1, 2, 3):
        pl.semaphore_signal(barrier, inc=1, device_id=device(x, shift(y, d), z, c), device_id_type=MESH)
    pl.semaphore_wait(barrier, 34)

    def along_a(d):
        return jnp.where(first, shift(x, d), x), jnp.where(first, z, shift(z, d))

    def along_b(d):
        return jnp.where(first, x, shift(x, d)), jnp.where(first, shift(z, d), z)

    def block_of(da, db):
        return jnp.where(first, shift(x, da), shift(x, db)), jnp.where(first, shift(z, db), shift(z, da))

    def send_block(xx, zz, to, half=None):
        ref = act_block(xx, zz, c)
        if half is not None:
            ref = ref.at[pl.ds(half * ROWS, ROWS), :]
        send(ref, ref, act_ss, act_rs.at[zz * SIDE + xx], device(to[0], y, to[1], c))

    def share_block(xx, zz):
        ref = act_block(xx, zz, c)
        send(ref, ref, act_ss, act_fs, sibling)

    def await_block(da, db):
        xx, zz = block_of(da, db)
        wait_bytes(act_block(xx, zz, c), act_rs.at[zz * SIDE + xx])
        return xx, zz

    loads[0].wait()
    for d in (1, 3):
        send_block(x, z, along_a(d))
        send_block(x, z, along_b(d))
    share_block(x, z)

    def around(i):
        return shift(x, lax.rem(i, SIDE)), shift(z, lax.rem(i // SIDE + i, SIDE))

    def send_weights(k):
        c0, cw = CHUNKS[k]
        target = wbuf.at[weight_rows(x, z, c), pl.ds(c0, cw)]

        def blend(p):
            cols = pl.ds(pl.multiple_of(p * UNITS + c0, 128), cw)
            for m in (0, 1):
                mix[m, :, cols] = mixed(mix[m, :, cols], old[m, :, cols])
            return cols

        own = blend(chip)
        pltpu.make_async_copy(mix.at[c, :, own], target, w_rs.at[k]).start()
        send(mix.at[1 - c, :, own], target, w_ss.at[k], w_rs.at[k], sibling)

        def one(i, carry):
            xx, zz = around(i)
            cols = blend(zz * SIDE + xx)
            for m in (0, 1):
                send(mix.at[m, :, cols], target, w_ss.at[k], w_rs.at[k], device(xx, y, zz, m))
            return carry

        lax.fori_loop(1, CHIPS, one, 0)

    for copy in loads[1:5]:
        copy.wait()
    send_weights(0)

    for s, da in ((0, 3), (1, 1), (None, 2)):
        xx, zz = await_block(da, 0)
        if s is not None:
            send_block(xx, zz, along_a((1, 3)[s]), s)
        for d in (1, 3):
            send_block(xx, zz, along_b(d))
        share_block(xx, zz)
    for da in (0, 3, 1, 2):
        for s, db in ((0, 3), (1, 1)):
            xx, zz = await_block(da, db)
            send_block(xx, zz, along_b((1, 3)[s]), s)
            share_block(xx, zz)

    send_weights(1)

    for copy in loads[5:]:
        copy.wait()

    def blend_down(i, carry):
        cols = pl.ds(pl.multiple_of(i * UNITS, 128), UNITS)
        mix[2, :, cols] = mixed(mix[2, :, cols], old[2, :, cols])
        return carry

    lax.fori_loop(0, CHIPS, blend_down, 0)

    def send_down():
        target = dbuf.at[weight_rows(x, z, c), :]
        cols = pl.ds(pl.multiple_of(chip * UNITS, 128), UNITS)
        pltpu.make_async_copy(mix.at[2, :, cols], target, d_rs.at[chip]).start()

        def one(i, carry):
            xx, zz = around(i)
            cols = pl.ds(pl.multiple_of((zz * SIDE + xx) * UNITS, 128), UNITS)
            send(mix.at[2, :, cols], target, d_ss, d_rs.at[chip], device(xx, y, zz, c))
            return carry

        lax.fori_loop(1, CHIPS, one, 0)

    def share_down():
        def one(i, carry):
            xx, zz = around(i)
            ref = dbuf.at[weight_rows(xx, zz, c), :]
            wait_bytes(ref, d_rs.at[zz * SIDE + xx])
            send(ref, ref, d_ss, d_fs, sibling)
            return carry

        lax.fori_loop(0, CHIPS, one, 0)

    for da in (0, 3, 1, 2):
        share_block(*await_block(da, 2))
    wait_bytes(act.at[pl.ds(0, TOKENS // 2), :], act_fs)

    def half_of(q, s):
        return pl.ds(pl.multiple_of(q * QUARTER + s * HALF, HALF), HALF)

    def multiply(k, *then):
        c0, cw = CHUNKS[k]
        cols = pl.ds(c0, cw)
        wait_bytes(wbuf.at[:, cols], w_rs.at[k])
        for act_now in then:
            act_now()

        def one(i, carry):
            q = shift(y, jnp.where(i == 0, 2, jnp.where(i == 3, 0, 2 * i - 1)))
            rows = pl.ds(pl.multiple_of(q * QUARTER, QUARTER), QUARTER)
            part[rows, cols] = jnp.dot(act[rows, :], wbuf[:, cols], preferred_element_type=F32).astype(BF16)

            @pl.when(i == 0)
            def _():
                for s, d in ((0, 1), (1, 3)):
                    send(part.at[half_of(q, s), cols], rl.at[s, :, cols], r_ss, r_rl.at[k, s], device(x, shift(y, d), z, c))

            for s in (0, 1):

                @pl.when(i == s + 1)
                def _():
                    o = 1 - s
                    send(part.at[half_of(q, o), cols], rf.at[s, pl.ds(o * HALF, HALF), cols], r_ss, r_rf.at[k, s], device(x, q, z, c))

            return carry

        lax.fori_loop(0, SIDE, one, 0)

    def relay(k):
        c0, cw = CHUNKS[k]
        cols = pl.ds(c0, cw)
        for s, d in ((0, 1), (1, 3)):
            q = shift(y, d)
            rows = half_of(q, s)
            wait_bytes(rl.at[s, :, cols], r_rl.at[k, s])
            part[rows, cols] = (part[rows, cols].astype(F32) + rl[s, :, cols].astype(F32)).astype(BF16)
            send(part.at[rows, cols], rf.at[s, pl.ds(s * HALF, HALF), cols], r_ss, r_rf.at[k, s], device(x, q, z, c))

    def reduce(k):
        c0, cw = CHUNKS[k]
        cols = pl.ds(c0, cw)
        for s in (0, 1):
            wait_bytes(rf.at[s, :, cols], r_rf.at[k, s])

        def one(j, carry):
            rows = pl.ds(pl.multiple_of(j * BLOCK, BLOCK), BLOCK)
            total = part[pl.ds(pl.multiple_of(y * QUARTER + j * BLOCK, BLOCK), BLOCK), cols].astype(F32)
            xs[rows, cols] = total + rf[0, rows, cols].astype(F32) + rf[1, rows, cols].astype(F32)
            return carry

        lax.fori_loop(0, SIDE, one, 0)
        for j in (0, 1):
            rows = pl.ds(pl.multiple_of((2 * j + 1 - c) * BLOCK, BLOCK), BLOCK)
            send(xs.at[rows, cols], xr.at[pl.ds(j * BLOCK, BLOCK), cols], x_ss, x_rs.at[k], sibling)

    def activate(k):
        c0, cw = CHUNKS[k]
        cols = pl.ds(c0, cw)
        wait_bytes(xr.at[:, cols], x_rs.at[k])
        for j in (0, 1):
            own = xs[pl.ds(pl.multiple_of((2 * j + c) * BLOCK, BLOCK), BLOCK), cols]
            other = xr[pl.ds(j * BLOCK, BLOCK), cols]
            gate, up = jnp.where(first, own, other), jnp.where(first, other, own)
            hid[pl.ds(pl.multiple_of((y * 2 + j) * BLOCK, BLOCK), BLOCK), cols] = (jax.nn.silu(gate) * up).astype(BF16)
        ref = hid.at[pl.ds(pl.multiple_of(y * HALF, HALF), HALF), cols]
        for s, d in ((0, 1), (1, 3)):
            send(ref, ref, h_ss, h_rs.at[k, s], device(x, shift(y, d), z, c))

    def forward(k):
        c0, cw = CHUNKS[k]
        cols = pl.ds(c0, cw)
        for s, d in ((0, 1), (1, 3)):
            q = shift(y, SIDE - d)
            wait_bytes(hid.at[pl.ds(pl.multiple_of(q * HALF, HALF), HALF), cols], h_rs.at[k, s])
            ref = hid.at[pl.ds(pl.multiple_of(q * HALF + s * BLOCK, BLOCK), BLOCK), cols]
            send(ref, ref, h_ss, h_ro.at[k], device(x, shift(y, d), z, c))

    multiply(0, lambda: send_weights(2))
    relay(0)
    multiply(1, lambda: send_weights(3))
    reduce(0)
    relay(1)
    activate(0)
    multiply(2)
    reduce(1)
    forward(0)
    relay(2)
    activate(1)
    multiply(3, send_down)
    reduce(2)
    forward(1)
    relay(3)
    activate(2)
    reduce(3)
    forward(2)
    activate(3)
    forward(3)
    share_down()
    wait_bytes(dbuf.at[pl.ds(0, PLANE // 2), :], d_fs)
    for k, (c0, cw) in enumerate(CHUNKS):
        wait_bytes(hid.at[pl.ds(0, HALF), pl.ds(c0, cw)], h_ro.at[k])

    a, b = jnp.where(first, z, x), jnp.where(first, x, z)
    first_to = [device(along_b(d)[0], y, along_b(d)[1], c) for d in (1, 3)]
    second_to = [device(along_a(d)[0], y, along_a(d)[1], c) for d in (1, 3)]
    ends = pl.ds(0, ROWS), pl.ds(ROWS, ROWS)

    def product(rows, n, width):
        tile = dbuf[pl.ds(pl.multiple_of(n * width, width), width), :]
        return lax.dot_general(rows, tile, (((1,), (1,)), ((), ())), preferred_element_type=F32).astype(BF16)

    def project(j):
        to = shift(b, (2, 1, 3, 0)[j])

        @pl.when(first)
        def _():
            rows = jnp.concatenate(
                [hid[pl.ds(pl.multiple_of((i * 2 + to // 2) * BLOCK, BLOCK), BLOCK), :] for i in range(SIDE)], axis=0
            )

            def one(n, carry):
                made = product(rows, lax.rem(to, 2) * 2 + n, 512)
                for i in range(SIDE):
                    ob[j, i, :, pl.ds(pl.multiple_of(n * 512, 512), 512)] = made[i * BLOCK : (i + 1) * BLOCK]
                return carry

            lax.fori_loop(0, 2, one, 0)

        @pl.when(c == 1)
        def _():
            def one(n, carry):
                made = product(hid[pl.ds(pl.multiple_of(to * HALF, HALF), HALF), :], n, FEATS)
                for h in (0, 1):
                    ob[j, h * 2 + n] = made[h * BLOCK : (h + 1) * BLOCK]
                return carry

            lax.fori_loop(0, 2, one, 0)

        for s, d in ((0, 1), (1, 3)):
            send(ob.at[j, shift(a, 2), ends[s]], o1l.at[j, s], o1_ss, o1_rl.at[j, s], first_to[s])
        for s, d in ((0, 1), (1, 3)):
            send(ob.at[j, shift(a, d), ends[1 - s]], o1f.at[j, s, ends[1 - s]], o1_ss, o1_rf.at[j, s], first_to[s])

    def pass_on(j):
        for s, d in ((0, 1), (1, 3)):
            i = shift(a, d)
            wait_bytes(o1l.at[j, s], o1_rl.at[j, s])
            ob[j, i, ends[s]] = (ob[j, i, ends[s]].astype(F32) + o1l[j, s].astype(F32)).astype(BF16)
            send(ob.at[j, i, ends[s]], o1f.at[j, s, ends[s]], o1_ss, o1_rf.at[j, s], first_to[s])

    def added(j):
        for s in (0, 1):
            wait_bytes(o1f.at[j, s], o1_rf.at[j, s])
        return ob[j, a].astype(F32) + o1f[j, 0].astype(F32) + o1f[j, 1].astype(F32)

    project(0)
    project(1)
    project(2)
    pass_on(0)
    project(3)
    pass_on(1)
    o2s[0] = added(0).astype(BF16)
    for s in (0, 1):
        send(o2s.at[0, ends[s]], o2l.at[s], o2_ss, o2_rl.at[s], second_to[s])
    pass_on(2)
    o2s[1] = added(1).astype(BF16)
    send(o2s.at[1, ends[1]], o2f.at[0, ends[1]], o2_ss, o2_rf.at[0], second_to[0])
    pass_on(3)
    o2s[2] = added(2).astype(BF16)
    send(o2s.at[2, ends[0]], o2f.at[1, ends[0]], o2_ss, o2_rf.at[1], second_to[1])
    for s in (0, 1):
        wait_bytes(o2l.at[s], o2_rl.at[s])
        o2s[s + 1, ends[s]] = (o2s[s + 1, ends[s]].astype(F32) + o2l[s].astype(F32)).astype(BF16)
        send(o2s.at[s + 1, ends[s]], o2f.at[s, ends[s]], o2_ss, o2_rf.at[s], second_to[s])
    total = added(3)
    for s in (0, 1):
        wait_bytes(o2f.at[s], o2_rf.at[s])
        total = total + o2f[s].astype(F32)
    out[...] = total.astype(BF16)

    wait_bytes(act.at[pl.ds(0, 31 * ROWS), :], act_ss)
    for k, (c0, cw) in enumerate(CHUNKS):
        wait_bytes(wbuf.at[pl.ds(0, 31 * ROWS), pl.ds(c0, cw)], w_ss.at[k])
    wait_bytes(dbuf.at[pl.ds(0, 31 * ROWS), :], d_ss)
    wait_bytes(part.at[pl.ds(0, 3 * QUARTER), :], r_ss)
    wait_bytes(xr, x_ss)
    wait_bytes(hid.at[pl.ds(0, 6 * BLOCK), :], h_ss)
    wait_bytes(ob.at[pl.ds(0, 3)], o1_ss)
    wait_bytes(o2s, o2_ss)


def per_device(activ, policy_gate, policy_up, policy_down, old_gate, old_up, old_down):
    sem = pltpu.SemaphoreType.DMA
    n = len(CHUNKS)
    return pl.pallas_call(
        kernel,
        name="layer",
        out_shape=jax.ShapeDtypeStruct((BLOCK, FEATS), BF16),
        in_specs=[pl.BlockSpec(memory_space=pl.ANY)] * 7,
        out_specs=pl.BlockSpec(memory_space=pltpu.VMEM),
        scratch_shapes=[
            pltpu.VMEM((3, ROWS, CHIPS * UNITS), BF16),
            pltpu.VMEM((3, ROWS, CHIPS * UNITS), BF16),
            pltpu.VMEM((TOKENS, PLANE), BF16),
            pltpu.VMEM((PLANE, UNITS), BF16),
            pltpu.VMEM((PLANE, UNITS), BF16),
            pltpu.VMEM((TOKENS, UNITS), BF16),
            pltpu.VMEM((2, HALF, UNITS), BF16),
            pltpu.VMEM((2, QUARTER, UNITS), BF16),
            pltpu.VMEM((QUARTER, UNITS), F32),
            pltpu.VMEM((2 * BLOCK, UNITS), F32),
            pltpu.VMEM((8 * BLOCK, UNITS), BF16),
            pltpu.VMEM((SIDE, SIDE, BLOCK, FEATS), BF16),
            pltpu.VMEM((SIDE, 2, ROWS, FEATS), BF16),
            pltpu.VMEM((SIDE, 2, BLOCK, FEATS), BF16),
            pltpu.VMEM((3, BLOCK, FEATS), BF16),
            pltpu.VMEM((2, ROWS, FEATS), BF16),
            pltpu.VMEM((2, BLOCK, FEATS), BF16),
            sem((7,)),
            sem, sem((CHIPS,)), sem,
            sem((n,)), sem((n,)),
            sem, sem((CHIPS,)), sem,
            sem, sem((n, 2)), sem((n, 2)),
            sem, sem((n,)),
            sem, sem((n, 2)), sem((n,)),
            sem, sem((SIDE, 2)), sem((SIDE, 2)),
            sem, sem((2,)), sem((2,)),
        ],
        compiler_params=pltpu.CompilerParams(
            collective_id=0, has_side_effects=True, vmem_limit_bytes=60 << 20
        ),
    )(activ, policy_gate, policy_up, policy_down.T, old_gate, old_up, old_down.T)


def solution(mesh):
    in_specs = (
        P("tp", "fsdp"),
        P(("fsdp", "tp"), None),
        P(("fsdp", "tp"), None),
        P(None, ("fsdp", "tp")),
        P(("fsdp", "tp"), None),
        P(("fsdp", "tp"), None),
        P(None, ("fsdp", "tp")),
    )
    return jax.shard_map(
        per_device, mesh=mesh, in_specs=in_specs, out_specs=P("tp", "fsdp"), check_vma=False
    )
```

```python
import functools

import jax
import jax.numpy as jnp
from jax import lax
from jax.experimental import pallas as pl
from jax.experimental.pallas import tpu as pltpu
from jax.sharding import PartitionSpec as P

MESH = pl.DeviceIdType.MESH
F32, BF16 = jnp.float32, jnp.bfloat16

SIDE = 4
CHIPS = 16
ROWS = 64
UNITS = 896
PLANE = 2048
TOKENS = 2048
QUARTER = 512
HALF = 256
BLOCK = 128
FEATS = 1024
CHUNKS = ((0, 128), (128, 128), (256, 128), (384, 128), (512, 128), (640, 128), (768, 128))

DOWN_PARTS = ((1, 8), (8, 16))


def device(x, y, z, c):
    return (y * 2 + x % 2, z * 4 + (x // 2) * 2 + c)


def shift(v, d):
    return lax.rem(v + d, SIDE)


def wait_bytes(ref, sem):
    pltpu.make_async_copy(ref, ref, sem).wait()


def mixed(a, b):
    return (0.6 * a.astype(F32) + 0.4 * b.astype(F32)).astype(BF16)


def kernel(
    act_in, pg_in, pu_in, pd_in, og_in, ou_in, od_in, out,
    mix, old, act, wbuf, dbuf, part, rl, rf, xs, xr, hid, ob, o1l, o1f, o2s, o2l, o2f,
    known, ld, act_ss, act_rs, act_fs, w_ss, w_rs, d_ss, d_rs, d_fs,
    r_ss, r_rl, r_rf, x_ss, x_rs, h_ss, h_rs, h_ro, o1_ss, o1_rl, o1_rf, o2_ss, o2_rl, o2_rf,
):
    f, t = lax.axis_index("fsdp"), lax.axis_index("tp")
    y, x_lo = f // 2, lax.rem(f, 2)
    z, x_hi, c = t // 4, lax.rem(t // 2, 2), lax.rem(t, 2)
    x = x_hi * 2 + x_lo
    first = c == 0
    chip = z * SIDE + x
    sibling = device(x, y, z, 1 - c)

    def send(src, dst, send_sem, recv_sem, to):
        pltpu.make_async_remote_copy(
            src_ref=src, dst_ref=dst, send_sem=send_sem, recv_sem=recv_sem, device_id=to, device_id_type=MESH
        ).start()

    def act_block(xx, zz, cc):
        tok = (zz * 4 + (xx // 2) * 2 + cc) * BLOCK
        return act.at[pl.ds(pl.multiple_of(tok, BLOCK), BLOCK), pl.ds(pl.multiple_of(lax.rem(xx, 2) * FEATS, FEATS), FEATS)]

    def weight_rows(xx, zz, cc):
        row = lax.rem(xx, 2) * FEATS + (zz * 2 + xx // 2) * 128 + cc * ROWS
        return pl.ds(pl.multiple_of(row, ROWS), ROWS)

    loads = [
        pltpu.make_async_copy(a, b, ld.at[i])
        for i, (a, b) in enumerate(
            [
                (act_in, act_block(x, z, c)),
                (pg_in, mix.at[0]), (og_in, old.at[0]),
                (pu_in, mix.at[1]), (ou_in, old.at[1]),
                (pd_in, mix.at[2]), (od_in, old.at[2]),
            ]
        )
    ]
    for copy in loads:
        copy.start()

    barrier = pltpu.get_barrier_semaphore()
    ring_x = [device(shift(x, d), y, z, c) for d in (1, 2, 3)]
    ring_z = [device(x, y, shift(z, d), c) for d in (1, 2, 3)]
    next_y = [device(x, shift(y, d), z, c) for d in (1, 3)]
    for to in (*ring_x, *ring_z, *next_y, sibling):
        pl.semaphore_signal(barrier, inc=1, device_id=to, device_id_type=MESH)
    pl.semaphore_wait(barrier, 9)

    def along_a(d):
        return jnp.where(first, shift(x, d), x), jnp.where(first, z, shift(z, d))

    def along_b(d):
        return jnp.where(first, x, shift(x, d)), jnp.where(first, shift(z, d), z)

    def block_of(da, db):
        return jnp.where(first, shift(x, da), shift(x, db)), jnp.where(first, shift(z, db), shift(z, da))

    def send_block(xx, zz, to, half=None):
        ref = act_block(xx, zz, c)
        if half is not None:
            ref = ref.at[pl.ds(half * ROWS, ROWS), :]
        send(ref, ref, act_ss, act_rs.at[zz * SIDE + xx], device(to[0], y, to[1], c))

    def share_block(xx, zz):
        ref = act_block(xx, zz, c)
        send(ref, ref, act_ss, act_fs, sibling)

    def await_block(da, db):
        xx, zz = block_of(da, db)
        wait_bytes(act_block(xx, zz, c), act_rs.at[zz * SIDE + xx])
        return xx, zz

    loads[0].wait()
    for d in (1, 3):
        send_block(x, z, along_a(d))
        send_block(x, z, along_b(d))
    share_block(x, z)

    for to in ring_z:
        pl.semaphore_signal(known.at[0], inc=1, device_id=to, device_id_type=MESH)
    pl.semaphore_wait(known.at[0], 3)
    pl.semaphore_signal(known.at[1], inc=1, device_id=sibling, device_id_type=MESH)
    pl.semaphore_wait(known.at[1], 1)

    def around(i):
        u, v = lax.rem(i, SIDE), lax.rem(i // SIDE + i, SIDE)
        return shift(x, jnp.where(first, u, v)), shift(z, jnp.where(first, v, u))

    def columns(p, c0, cw):
        return pl.ds(pl.multiple_of(p * UNITS + c0, 128), cw)

    def blend(m, p, c0, cw):
        cols = columns(p, c0, cw)
        mix[m, :, cols] = mixed(mix[m, :, cols], old[m, :, cols])

    def send_weights(k, then=None):
        c0, cw = CHUNKS[k]
        target = wbuf.at[weight_rows(x, z, c), pl.ds(c0, cw)]
        if then:
            then(chip)
        own = columns(chip, c0, cw)
        pltpu.make_async_copy(mix.at[c, :, own], target, w_rs.at[k]).start()
        send(mix.at[1 - c, :, own], target, w_ss.at[k], w_rs.at[k], sibling)

        def one(i, carry):
            xx, zz = around(i)
            p = zz * SIDE + xx
            if then:
                then(p)
            for m in (0, 1):
                send(mix.at[m, :, columns(p, c0, cw)], target, w_ss.at[k], w_rs.at[k], device(xx, y, zz, m))
            return carry

        lax.fori_loop(1, CHIPS, one, 0)

    def blend_first(p):
        for m in (0, 1):
            blend(m, p, *CHUNKS[0])

    def blend_rest(p, carry):
        for m in (0, 1):
            blend(m, p, CHUNKS[0][1], UNITS - CHUNKS[0][1])
        return carry

    def blend_down(p, carry):
        blend(2, p, 0, UNITS)
        return carry

    for copy in loads[1:5]:
        copy.wait()
    send_weights(0, blend_first)
    lax.fori_loop(0, CHIPS, blend_rest, 0)

    for s, da in ((0, 3), (1, 1), (None, 2)):
        xx, zz = await_block(da, 0)
        if s is not None:
            send_block(xx, zz, along_a((1, 3)[s]), s)
        for d in (1, 3):
            send_block(xx, zz, along_b(d))
        share_block(xx, zz)
    for da in (0, 3, 1, 2):
        for s, db in ((0, 3), (1, 1)):
            xx, zz = await_block(da, db)
            send_block(xx, zz, along_b((1, 3)[s]), s)
            share_block(xx, zz)

    send_weights(1)
    send_weights(2)

    for copy in loads[5:]:
        copy.wait()
    lax.fori_loop(0, CHIPS, blend_down, 0)

    def send_down(part):
        target = dbuf.at[weight_rows(x, z, c), :]
        if part == 0:
            pltpu.make_async_copy(mix.at[2, :, columns(chip, 0, UNITS)], target, d_rs.at[chip]).start()

        def one(i, carry):
            xx, zz = around(i)
            send(mix.at[2, :, columns(zz * SIDE + xx, 0, UNITS)], target, d_ss, d_rs.at[chip], device(xx, y, zz, c))
            return carry

        lax.fori_loop(*DOWN_PARTS[part], one, 0)

    def share_down():
        def one(i, carry):
            xx, zz = around(i)
            ref = dbuf.at[weight_rows(xx, zz, c), :]
            wait_bytes(ref, d_rs.at[zz * SIDE + xx])
            send(ref, ref, d_ss, d_fs, sibling)
            return carry

        lax.fori_loop(0, CHIPS, one, 0)

    for da in (0, 3, 1, 2):
        share_block(*await_block(da, 2))
    wait_bytes(act.at[pl.ds(0, TOKENS // 2), :], act_fs)

    def half_of(q, s):
        return pl.ds(pl.multiple_of(q * QUARTER + s * HALF, HALF), HALF)

    def multiply(k, *then):
        c0, cw = CHUNKS[k]
        cols = pl.ds(c0, cw)
        wait_bytes(wbuf.at[:, cols], w_rs.at[k])
        for step, n in then:
            step(n)

        def one(i, carry):
            q = shift(y, jnp.where(i == 0, 2, jnp.where(i == 3, 0, 2 * i - 1)))
            rows = pl.ds(pl.multiple_of(q * QUARTER, QUARTER), QUARTER)
            part[rows, cols] = jnp.dot(act[rows, :], wbuf[:, cols], preferred_element_type=F32).astype(BF16)

            @pl.when(i == 0)
            def _():
                for s, d in ((0, 1), (1, 3)):
                    send(part.at[half_of(q, s), cols], rl.at[s, :, cols], r_ss, r_rl.at[k, s], device(x, shift(y, d), z, c))

            for s in (0, 1):

                @pl.when(i == s + 1)
                def _():
                    o = 1 - s
                    send(part.at[half_of(q, o), cols], rf.at[s, pl.ds(o * HALF, HALF), cols], r_ss, r_rf.at[k, s], device(x, q, z, c))

            return carry

        lax.fori_loop(0, SIDE, one, 0)

    def relay(k):
        c0, cw = CHUNKS[k]
        cols = pl.ds(c0, cw)
        for s, d in ((0, 1), (1, 3)):
            q = shift(y, d)
            rows = half_of(q, s)
            wait_bytes(rl.at[s, :, cols], r_rl.at[k, s])
            part[rows, cols] = (part[rows, cols].astype(F32) + rl[s, :, cols].astype(F32)).astype(BF16)
            send(part.at[rows, cols], rf.at[s, pl.ds(s * HALF, HALF), cols], r_ss, r_rf.at[k, s], device(x, q, z, c))

    def reduce(k):
        c0, cw = CHUNKS[k]
        cols = pl.ds(c0, cw)
        for s in (0, 1):
            wait_bytes(rf.at[s, :, cols], r_rf.at[k, s])

        def one(j, carry):
            rows = pl.ds(pl.multiple_of(j * BLOCK, BLOCK), BLOCK)
            total = part[pl.ds(pl.multiple_of(y * QUARTER + j * BLOCK, BLOCK), BLOCK), cols].astype(F32)
            xs[rows, cols] = total + rf[0, rows, cols].astype(F32) + rf[1, rows, cols].astype(F32)
            return carry

        lax.fori_loop(0, SIDE, one, 0)
        for j in (0, 1):
            rows = pl.ds(pl.multiple_of((2 * j + 1 - c) * BLOCK, BLOCK), BLOCK)
            send(xs.at[rows, cols], xr.at[pl.ds(j * BLOCK, BLOCK), cols], x_ss, x_rs.at[k], sibling)

    def activate(k):
        c0, cw = CHUNKS[k]
        cols = pl.ds(c0, cw)
        wait_bytes(xr.at[:, cols], x_rs.at[k])
        for j in (0, 1):
            own = xs[pl.ds(pl.multiple_of((2 * j + c) * BLOCK, BLOCK), BLOCK), cols]
            other = xr[pl.ds(j * BLOCK, BLOCK), cols]
            gate, up = jnp.where(first, own, other), jnp.where(first, other, own)
            hid[pl.ds(pl.multiple_of((y * 2 + j) * BLOCK, BLOCK), BLOCK), cols] = (jax.nn.silu(gate) * up).astype(BF16)
        ref = hid.at[pl.ds(pl.multiple_of(y * HALF, HALF), HALF), cols]
        for s, d in ((0, 1), (1, 3)):
            send(ref, ref, h_ss, h_rs.at[k, s], device(x, shift(y, d), z, c))

    def forward(k):
        c0, cw = CHUNKS[k]
        cols = pl.ds(c0, cw)
        for s, d in ((0, 1), (1, 3)):
            q = shift(y, SIDE - d)
            wait_bytes(hid.at[pl.ds(pl.multiple_of(q * HALF, HALF), HALF), cols], h_rs.at[k, s])
            ref = hid.at[pl.ds(pl.multiple_of(q * HALF + s * BLOCK, BLOCK), BLOCK), cols]
            send(ref, ref, h_ss, h_ro.at[k], device(x, shift(y, d), z, c))

    multiply(0, (send_weights, 3))
    multiply(1, (send_weights, 4))
    relay(0)
    multiply(2, (send_weights, 5))
    relay(1)
    reduce(0)
    multiply(3, (send_weights, 6))
    relay(2)
    reduce(1)
    activate(0)
    multiply(4)
    relay(3)
    reduce(2)
    activate(1)
    forward(0)
    multiply(5, (send_down, 0), (send_down, 1))
    relay(4)
    reduce(3)
    activate(2)
    forward(1)
    multiply(6)
    relay(5)
    reduce(4)
    activate(3)
    forward(2)
    relay(6)
    reduce(5)
    activate(4)
    forward(3)
    reduce(6)
    activate(5)
    forward(4)
    activate(6)
    forward(5)
    forward(6)
    share_down()
    wait_bytes(dbuf.at[pl.ds(0, PLANE // 2), :], d_fs)
    for k, (c0, cw) in enumerate(CHUNKS):
        wait_bytes(hid.at[pl.ds(0, HALF), pl.ds(c0, cw)], h_ro.at[k])

    a, b = jnp.where(first, z, x), jnp.where(first, x, z)
    first_to = [device(along_b(d)[0], y, along_b(d)[1], c) for d in (1, 3)]
    second_to = [device(along_a(d)[0], y, along_a(d)[1], c) for d in (1, 3)]
    ends = pl.ds(0, ROWS), pl.ds(ROWS, ROWS)

    def product(rows, n, width):
        tile = dbuf[pl.ds(pl.multiple_of(n * width, width), width), :]
        return lax.dot_general(rows, tile, (((1,), (1,)), ((), ())), preferred_element_type=F32).astype(BF16)

    def project(j):
        to = shift(b, (2, 1, 3, 0)[j])

        @pl.when(first)
        def _():
            rows = jnp.concatenate(
                [hid[pl.ds(pl.multiple_of((i * 2 + to // 2) * BLOCK, BLOCK), BLOCK), :] for i in range(SIDE)], axis=0
            )

            def one(n, carry):
                made = product(rows, lax.rem(to, 2) * 2 + n, 512)
                for i in range(SIDE):
                    ob[j, i, :, pl.ds(pl.multiple_of(n * 512, 512), 512)] = made[i * BLOCK : (i + 1) * BLOCK]
                return carry

            lax.fori_loop(0, 2, one, 0)

        @pl.when(c == 1)
        def _():
            def one(n, carry):
                made = product(hid[pl.ds(pl.multiple_of(to * HALF, HALF), HALF), :], n, FEATS)
                for h in (0, 1):
                    ob[j, h * 2 + n] = made[h * BLOCK : (h + 1) * BLOCK]
                return carry

            lax.fori_loop(0, 2, one, 0)

    def emit(j):
        for s, d in ((0, 1), (1, 3)):
            send(ob.at[j, shift(a, 2), ends[s]], o1l.at[j, s], o1_ss, o1_rl.at[j, s], first_to[s])
        for s, d in ((0, 1), (1, 3)):
            send(ob.at[j, shift(a, d), ends[1 - s]], o1f.at[j, s, ends[1 - s]], o1_ss, o1_rf.at[j, s], first_to[s])

    def pass_on(j):
        for s, d in ((0, 1), (1, 3)):
            i = shift(a, d)
            wait_bytes(o1l.at[j, s], o1_rl.at[j, s])
            ob[j, i, ends[s]] = (ob[j, i, ends[s]].astype(F32) + o1l[j, s].astype(F32)).astype(BF16)
            send(ob.at[j, i, ends[s]], o1f.at[j, s, ends[s]], o1_ss, o1_rf.at[j, s], first_to[s])

    def added(j):
        for s in (0, 1):
            wait_bytes(o1f.at[j, s], o1_rf.at[j, s])
        return ob[j, a].astype(F32) + o1f[j, 0].astype(F32) + o1f[j, 1].astype(F32)

    def finish(j):
        o2s[j] = added(j).astype(BF16)
        if j == 0:
            for s in (0, 1):
                send(o2s.at[0, ends[s]], o2l.at[s], o2_ss, o2_rl.at[s], second_to[s])
        else:
            s = j - 1
            send(o2s.at[j, ends[1 - s]], o2f.at[s, ends[1 - s]], o2_ss, o2_rf.at[s], second_to[s])

    def finish_far():
        for s in (0, 1):
            wait_bytes(o2l.at[s], o2_rl.at[s])
            o2s[s + 1, ends[s]] = (o2s[s + 1, ends[s]].astype(F32) + o2l[s].astype(F32)).astype(BF16)
            send(o2s.at[s + 1, ends[s]], o2f.at[s, ends[s]], o2_ss, o2_rf.at[s], second_to[s])

    project(0)
    emit(0)
    project(1)
    emit(1)
    project(2)
    emit(2)
    pass_on(0)
    project(3)
    emit(3)
    pass_on(1)
    finish(0)
    pass_on(2)
    finish(1)
    pass_on(3)
    finish(2)
    finish_far()
    total = added(3)
    for s in (0, 1):
        wait_bytes(o2f.at[s], o2_rf.at[s])
        total = total + o2f[s].astype(F32)
    out[...] = total.astype(BF16)

    wait_bytes(act.at[pl.ds(0, 31 * ROWS), :], act_ss)
    for k, (c0, cw) in enumerate(CHUNKS):
        wait_bytes(wbuf.at[pl.ds(0, 31 * ROWS), pl.ds(c0, cw)], w_ss.at[k])
    wait_bytes(dbuf.at[pl.ds(0, 31 * ROWS), :], d_ss)
    wait_bytes(part.at[pl.ds(0, 3 * QUARTER), :], r_ss)
    wait_bytes(xr, x_ss)
    wait_bytes(hid.at[pl.ds(0, 6 * BLOCK), :], h_ss)
    wait_bytes(ob.at[pl.ds(0, 3)], o1_ss)
    wait_bytes(o2s, o2_ss)


def per_device(activ, policy_gate, policy_up, policy_down, old_gate, old_up, old_down):
    sem = pltpu.SemaphoreType.DMA
    n = len(CHUNKS)
    return pl.pallas_call(
        kernel,
        name="layer",
        out_shape=jax.ShapeDtypeStruct((BLOCK, FEATS), BF16),
        in_specs=[pl.BlockSpec(memory_space=pl.ANY)] * 7,
        out_specs=pl.BlockSpec(memory_space=pltpu.VMEM),
        scratch_shapes=[
            pltpu.VMEM((3, ROWS, CHIPS * UNITS), BF16),
            pltpu.VMEM((3, ROWS, CHIPS * UNITS), BF16),
            pltpu.VMEM((TOKENS, PLANE), BF16),
            pltpu.VMEM((PLANE, UNITS), BF16),
            pltpu.VMEM((PLANE, UNITS), BF16),
            pltpu.VMEM((TOKENS, UNITS), BF16),
            pltpu.VMEM((2, HALF, UNITS), BF16),
            pltpu.VMEM((2, QUARTER, UNITS), BF16),
            pltpu.VMEM((QUARTER, UNITS), F32),
            pltpu.VMEM((2 * BLOCK, UNITS), F32),
            pltpu.VMEM((8 * BLOCK, UNITS), BF16),
            pltpu.VMEM((SIDE, SIDE, BLOCK, FEATS), BF16),
            pltpu.VMEM((SIDE, 2, ROWS, FEATS), BF16),
            pltpu.VMEM((SIDE, 2, BLOCK, FEATS), BF16),
            pltpu.VMEM((3, BLOCK, FEATS), BF16),
            pltpu.VMEM((2, ROWS, FEATS), BF16),
            pltpu.VMEM((2, BLOCK, FEATS), BF16),
            pltpu.SemaphoreType.REGULAR((2,)),
            sem((7,)),
            sem, sem((CHIPS,)), sem,
            sem((n,)), sem((n,)),
            sem, sem((CHIPS,)), sem,
            sem, sem((n, 2)), sem((n, 2)),
            sem, sem((n,)),
            sem, sem((n, 2)), sem((n,)),
            sem, sem((SIDE, 2)), sem((SIDE, 2)),
            sem, sem((2,)), sem((2,)),
        ],
        compiler_params=pltpu.CompilerParams(
            collective_id=0, has_side_effects=True, vmem_limit_bytes=60 << 20
        ),
    )(activ, policy_gate, policy_up, policy_down.T, old_gate, old_up, old_down.T)


def solution(mesh):
    in_specs = (
        P("tp", "fsdp"),
        P(("fsdp", "tp"), None),
        P(("fsdp", "tp"), None),
        P(None, ("fsdp", "tp")),
        P(("fsdp", "tp"), None),
        P(("fsdp", "tp"), None),
        P(None, ("fsdp", "tp")),
    )
    return jax.shard_map(
        per_device, mesh=mesh, in_specs=in_specs, out_specs=P("tp", "fsdp"), check_vma=False
    )
```

```python
import functools

import jax
import jax.numpy as jnp
from jax import lax
from jax.experimental import pallas as pl
from jax.experimental.pallas import tpu as pltpu
from jax.sharding import PartitionSpec as P

MESH = pl.DeviceIdType.MESH
F32, BF16 = jnp.float32, jnp.bfloat16

SIDE = 4
CHIPS = 16
ROWS = 64
UNITS = 896
PLANE = 2048
TOKENS = 2048
QUARTER = 512
HALF = 256
BLOCK = 128
FEATS = 1024
CHUNKS = ((0, 128), (128, 128), (256, 128), (384, 128), (512, 128), (640, 128), (768, 128))

DOWN_PARTS = ((1, 8), (8, 16))


def device(x, y, z, c):
    return (y * 2 + x % 2, z * 4 + (x // 2) * 2 + c)


def shift(v, d):
    return lax.rem(v + d, SIDE)


def wait_bytes(ref, sem):
    pltpu.make_async_copy(ref, ref, sem).wait()


def mixed(a, b):
    return (0.6 * a.astype(F32) + 0.4 * b.astype(F32)).astype(BF16)


def kernel(
    act_in, pg_in, pu_in, pd_in, og_in, ou_in, od_in, out,
    mix, old, act, wbuf, dbuf, part, rl, rf, xs, xr, hid, ob, o1l, o1f, o2s, o2l, o2f,
    known, ld, act_ss, act_rs, act_fs, w_ss, w_rs, d_ss, d_rs, d_fs,
    r_ss, r_rl, r_rf, x_ss, x_rs, h_ss, h_rs, h_ro, o1_ss, o1_rl, o1_rf, o2_ss, o2_rl, o2_rf,
):
    f, t = lax.axis_index("fsdp"), lax.axis_index("tp")
    y, x_lo = f // 2, lax.rem(f, 2)
    z, x_hi, c = t // 4, lax.rem(t // 2, 2), lax.rem(t, 2)
    x = x_hi * 2 + x_lo
    first = c == 0
    chip = z * SIDE + x
    sibling = device(x, y, z, 1 - c)

    def send(src, dst, send_sem, recv_sem, to):
        pltpu.make_async_remote_copy(
            src_ref=src, dst_ref=dst, send_sem=send_sem, recv_sem=recv_sem, device_id=to, device_id_type=MESH
        ).start()

    def act_block(xx, zz, cc):
        tok = (zz * 4 + (xx // 2) * 2 + cc) * BLOCK
        return act.at[pl.ds(pl.multiple_of(tok, BLOCK), BLOCK), pl.ds(pl.multiple_of(lax.rem(xx, 2) * FEATS, FEATS), FEATS)]

    def weight_rows(xx, zz, cc):
        row = lax.rem(xx, 2) * FEATS + (zz * 2 + xx // 2) * 128 + cc * ROWS
        return pl.ds(pl.multiple_of(row, ROWS), ROWS)

    loads = [
        pltpu.make_async_copy(a, b, ld.at[i])
        for i, (a, b) in enumerate(
            [
                (act_in, act_block(x, z, c)),
                (pg_in, mix.at[0]), (og_in, old.at[0]),
                (pu_in, mix.at[1]), (ou_in, old.at[1]),
                (pd_in, mix.at[2]), (od_in, old.at[2]),
            ]
        )
    ]
    for copy in loads:
        copy.start()

    barrier = pltpu.get_barrier_semaphore()
    ring_x = [device(shift(x, d), y, z, c) for d in (1, 2, 3)]
    ring_z = [device(x, y, shift(z, d), c) for d in (1, 2, 3)]
    next_y = [device(x, shift(y, d), z, c) for d in (1, 3)]
    for to in (*ring_x, *ring_z, *next_y, sibling):
        pl.semaphore_signal(barrier, inc=1, device_id=to, device_id_type=MESH)
    pl.semaphore_wait(barrier, 9)

    def along_a(d):
        return jnp.where(first, shift(x, d), x), jnp.where(first, z, shift(z, d))

    def along_b(d):
        return jnp.where(first, x, shift(x, d)), jnp.where(first, shift(z, d), z)

    def block_of(da, db):
        return jnp.where(first, shift(x, da), shift(x, db)), jnp.where(first, shift(z, db), shift(z, da))

    def send_block(xx, zz, to, half=None):
        ref = act_block(xx, zz, c)
        if half is not None:
            ref = ref.at[pl.ds(half * ROWS, ROWS), :]
        send(ref, ref, act_ss, act_rs.at[zz * SIDE + xx], device(to[0], y, to[1], c))

    def share_block(xx, zz):
        ref = act_block(xx, zz, c)
        send(ref, ref, act_ss, act_fs, sibling)

    def await_block(da, db):
        xx, zz = block_of(da, db)
        wait_bytes(act_block(xx, zz, c), act_rs.at[zz * SIDE + xx])
        return xx, zz

    loads[0].wait()
    for d in (1, 3):
        send_block(x, z, along_a(d))
        send_block(x, z, along_b(d))
    share_block(x, z)

    for to in ring_z:
        pl.semaphore_signal(known.at[0], inc=1, device_id=to, device_id_type=MESH)
    pl.semaphore_wait(known.at[0], 3)
    pl.semaphore_signal(known.at[1], inc=1, device_id=sibling, device_id_type=MESH)
    pl.semaphore_wait(known.at[1], 1)

    def around(i):
        u, v = lax.rem(i, SIDE), lax.rem(i // SIDE + i, SIDE)
        return shift(x, jnp.where(first, u, v)), shift(z, jnp.where(first, v, u))

    def columns(p, c0, cw):
        return pl.ds(pl.multiple_of(p * UNITS + c0, 128), cw)

    def blend(m, p, c0, cw):
        cols = columns(p, c0, cw)
        mix[m, :, cols] = mixed(mix[m, :, cols], old[m, :, cols])

    def send_weights(k, then=None):
        c0, cw = CHUNKS[k]
        target = wbuf.at[weight_rows(x, z, c), pl.ds(c0, cw)]
        if then:
            then(chip)
        own = columns(chip, c0, cw)
        pltpu.make_async_copy(mix.at[c, :, own], target, w_rs.at[k]).start()
        send(mix.at[1 - c, :, own], target, w_ss.at[k], w_rs.at[k], sibling)

        def one(i, carry):
            xx, zz = around(i)
            p = zz * SIDE + xx
            if then:
                then(p)
            for m in (0, 1):
                send(mix.at[m, :, columns(p, c0, cw)], target, w_ss.at[k], w_rs.at[k], device(xx, y, zz, m))
            return carry

        lax.fori_loop(1, CHIPS, one, 0)

    def blend_first(p):
        for m in (0, 1):
            blend(m, p, *CHUNKS[0])

    def blend_rest(p, carry):
        for m in (0, 1):
            blend(m, p, CHUNKS[0][1], UNITS - CHUNKS[0][1])
        return carry

    def blend_down(p, carry):
        blend(2, p, 0, UNITS)
        return carry

    for copy in loads[1:5]:
        copy.wait()
    send_weights(0, blend_first)
    lax.fori_loop(0, CHIPS, blend_rest, 0)

    for s, da in ((0, 3), (1, 1), (None, 2)):
        xx, zz = await_block(da, 0)
        if s is not None:
            send_block(xx, zz, along_a((1, 3)[s]), s)
        for d in (1, 3):
            send_block(xx, zz, along_b(d))
        share_block(xx, zz)
    for da in (0, 3, 1, 2):
        for s, db in ((0, 3), (1, 1)):
            xx, zz = await_block(da, db)
            send_block(xx, zz, along_b((1, 3)[s]), s)
            share_block(xx, zz)

    send_weights(1)
    send_weights(2)

    for copy in loads[5:]:
        copy.wait()
    lax.fori_loop(0, CHIPS, blend_down, 0)

    def send_down(part):
        target = dbuf.at[weight_rows(x, z, c), :]
        if part == 0:
            pltpu.make_async_copy(mix.at[2, :, columns(chip, 0, UNITS)], target, d_rs.at[chip]).start()

        def one(i, carry):
            xx, zz = around(i)
            send(mix.at[2, :, columns(zz * SIDE + xx, 0, UNITS)], target, d_ss, d_rs.at[chip], device(xx, y, zz, c))
            return carry

        lax.fori_loop(*DOWN_PARTS[part], one, 0)

    def share_down():
        def one(i, carry):
            xx, zz = around(i)
            ref = dbuf.at[weight_rows(xx, zz, c), :]
            wait_bytes(ref, d_rs.at[zz * SIDE + xx])
            send(ref, ref, d_ss, d_fs, sibling)
            return carry

        lax.fori_loop(0, CHIPS, one, 0)

    for da in (0, 3, 1, 2):
        share_block(*await_block(da, 2))
    wait_bytes(act.at[pl.ds(0, TOKENS // 2), :], act_fs)

    def half_of(q, s):
        return pl.ds(pl.multiple_of(q * QUARTER + s * HALF, HALF), HALF)

    def multiply(k, *then):
        c0, cw = CHUNKS[k]
        cols = pl.ds(c0, cw)
        wait_bytes(wbuf.at[:, cols], w_rs.at[k])
        for step, n in then:
            step(n)

        def one(i, carry):
            q = shift(y, jnp.where(i == 0, 2, jnp.where(i == 3, 0, 2 * i - 1)))
            rows = pl.ds(pl.multiple_of(q * QUARTER, QUARTER), QUARTER)
            part[rows, cols] = jnp.dot(act[rows, :], wbuf[:, cols], preferred_element_type=F32).astype(BF16)

            @pl.when(i == 0)
            def _():
                for s, d in ((0, 1), (1, 3)):
                    send(part.at[half_of(q, s), cols], rl.at[s, :, cols], r_ss, r_rl.at[k, s], device(x, shift(y, d), z, c))

            for s in (0, 1):

                @pl.when(i == s + 1)
                def _():
                    o = 1 - s
                    send(part.at[half_of(q, o), cols], rf.at[s, pl.ds(o * HALF, HALF), cols], r_ss, r_rf.at[k, s], device(x, q, z, c))

            return carry

        lax.fori_loop(0, SIDE, one, 0)

    def relay(k):
        c0, cw = CHUNKS[k]
        cols = pl.ds(c0, cw)
        for s, d in ((0, 1), (1, 3)):
            q = shift(y, d)
            rows = half_of(q, s)
            wait_bytes(rl.at[s, :, cols], r_rl.at[k, s])
            part[rows, cols] = (part[rows, cols].astype(F32) + rl[s, :, cols].astype(F32)).astype(BF16)
            send(part.at[rows, cols], rf.at[s, pl.ds(s * HALF, HALF), cols], r_ss, r_rf.at[k, s], device(x, q, z, c))

    def reduce(k):
        c0, cw = CHUNKS[k]
        cols = pl.ds(c0, cw)
        for s in (0, 1):
            wait_bytes(rf.at[s, :, cols], r_rf.at[k, s])

        def one(j, carry):
            rows = pl.ds(pl.multiple_of(j * BLOCK, BLOCK), BLOCK)
            total = part[pl.ds(pl.multiple_of(y * QUARTER + j * BLOCK, BLOCK), BLOCK), cols].astype(F32)
            xs[rows, cols] = total + rf[0, rows, cols].astype(F32) + rf[1, rows, cols].astype(F32)
            return carry

        lax.fori_loop(0, SIDE, one, 0)
        for j in (0, 1):
            rows = pl.ds(pl.multiple_of((2 * j + 1 - c) * BLOCK, BLOCK), BLOCK)
            send(xs.at[rows, cols], xr.at[pl.ds(j * BLOCK, BLOCK), cols], x_ss, x_rs.at[k], sibling)

    def activate(k):
        c0, cw = CHUNKS[k]
        cols = pl.ds(c0, cw)
        wait_bytes(xr.at[:, cols], x_rs.at[k])
        for j in (0, 1):
            own = xs[pl.ds(pl.multiple_of((2 * j + c) * BLOCK, BLOCK), BLOCK), cols]
            other = xr[pl.ds(j * BLOCK, BLOCK), cols]
            gate, up = jnp.where(first, own, other), jnp.where(first, other, own)
            hid[pl.ds(pl.multiple_of((y * 2 + j) * BLOCK, BLOCK), BLOCK), cols] = (jax.nn.silu(gate) * up).astype(BF16)
        ref = hid.at[pl.ds(pl.multiple_of(y * HALF, HALF), HALF), cols]
        for s, d in ((0, 1), (1, 3)):
            send(ref, ref, h_ss, h_rs.at[k, s], device(x, shift(y, d), z, c))

    def forward(k):
        c0, cw = CHUNKS[k]
        cols = pl.ds(c0, cw)
        for s, d in ((0, 1), (1, 3)):
            q = shift(y, SIDE - d)
            wait_bytes(hid.at[pl.ds(pl.multiple_of(q * HALF, HALF), HALF), cols], h_rs.at[k, s])
            ref = hid.at[pl.ds(pl.multiple_of(q * HALF + s * BLOCK, BLOCK), BLOCK), cols]
            send(ref, ref, h_ss, h_ro.at[k], device(x, shift(y, d), z, c))

    multiply(0, (send_weights, 3))
    multiply(1, (send_weights, 4))
    relay(0)
    multiply(2, (send_weights, 5))
    relay(1)
    reduce(0)
    multiply(3, (send_weights, 6))
    relay(2)
    reduce(1)
    activate(0)
    multiply(4)
    relay(3)
    reduce(2)
    activate(1)
    forward(0)
    multiply(5, (send_down, 0), (send_down, 1))
    relay(4)
    reduce(3)
    activate(2)
    forward(1)
    multiply(6)
    relay(5)
    reduce(4)
    activate(3)
    forward(2)
    relay(6)
    reduce(5)
    activate(4)
    forward(3)
    reduce(6)
    activate(5)
    forward(4)
    activate(6)
    forward(5)
    forward(6)
    share_down()
    wait_bytes(dbuf.at[pl.ds(0, PLANE // 2), :], d_fs)
    for k, (c0, cw) in enumerate(CHUNKS):
        wait_bytes(hid.at[pl.ds(0, HALF), pl.ds(c0, cw)], h_ro.at[k])

    a, b = jnp.where(first, z, x), jnp.where(first, x, z)
    first_to = [device(along_b(d)[0], y, along_b(d)[1], c) for d in (1, 3)]
    second_to = [device(along_a(d)[0], y, along_a(d)[1], c) for d in (1, 3)]
    ends = pl.ds(0, ROWS), pl.ds(ROWS, ROWS)

    def product(rows, n, width):
        tile = dbuf[pl.ds(pl.multiple_of(n * width, width), width), :]
        return lax.dot_general(rows, tile, (((1,), (1,)), ((), ())), preferred_element_type=F32).astype(BF16)

    def project(j):
        to = shift(b, (2, 1, 3, 0)[j])

        @pl.when(first)
        def _():
            rows = jnp.concatenate(
                [hid[pl.ds(pl.multiple_of((i * 2 + to // 2) * BLOCK, BLOCK), BLOCK), :] for i in range(SIDE)], axis=0
            )

            def one(n, carry):
                made = product(rows, lax.rem(to, 2) * 2 + n, 512)
                for i in range(SIDE):
                    ob[j, i, :, pl.ds(pl.multiple_of(n * 512, 512), 512)] = made[i * BLOCK : (i + 1) * BLOCK]
                return carry

            lax.fori_loop(0, 2, one, 0)

        @pl.when(c == 1)
        def _():
            def one(n, carry):
                made = product(hid[pl.ds(pl.multiple_of(to * HALF, HALF), HALF), :], n, FEATS)
                for h in (0, 1):
                    ob[j, h * 2 + n] = made[h * BLOCK : (h + 1) * BLOCK]
                return carry

            lax.fori_loop(0, 2, one, 0)

    def emit(j):
        for s, d in ((0, 1), (1, 3)):
            send(ob.at[j, shift(a, 2), ends[s]], o1l.at[j, s], o1_ss, o1_rl.at[j, s], first_to[s])
        for s, d in ((0, 1), (1, 3)):
            send(ob.at[j, shift(a, d), ends[1 - s]], o1f.at[j, s, ends[1 - s]], o1_ss, o1_rf.at[j, s], first_to[s])

    def pass_on(j):
        for s, d in ((0, 1), (1, 3)):
            i = shift(a, d)
            wait_bytes(o1l.at[j, s], o1_rl.at[j, s])
            ob[j, i, ends[s]] = (ob[j, i, ends[s]].astype(F32) + o1l[j, s].astype(F32)).astype(BF16)
            send(ob.at[j, i, ends[s]], o1f.at[j, s, ends[s]], o1_ss, o1_rf.at[j, s], first_to[s])

    def added(j):
        for s in (0, 1):
            wait_bytes(o1f.at[j, s], o1_rf.at[j, s])
        return ob[j, a].astype(F32) + o1f[j, 0].astype(F32) + o1f[j, 1].astype(F32)

    def finish(j):
        o2s[j] = added(j).astype(BF16)
        if j == 0:
            for s in (0, 1):
                send(o2s.at[0, ends[s]], o2l.at[s], o2_ss, o2_rl.at[s], second_to[s])
        else:
            s = j - 1
            send(o2s.at[j, ends[1 - s]], o2f.at[s, ends[1 - s]], o2_ss, o2_rf.at[s], second_to[s])

    def finish_far():
        for s in (0, 1):
            wait_bytes(o2l.at[s], o2_rl.at[s])
            o2s[s + 1, ends[s]] = (o2s[s + 1, ends[s]].astype(F32) + o2l[s].astype(F32)).astype(BF16)
            send(o2s.at[s + 1, ends[s]], o2f.at[s, ends[s]], o2_ss, o2_rf.at[s], second_to[s])

    project(0)
    emit(0)
    project(1)
    emit(1)
    project(2)
    emit(2)
    project(3)
    pass_on(0)
    pass_on(1)
    pass_on(2)
    emit(3)
    finish(0)
    finish(1)
    finish(2)
    pass_on(3)
    finish_far()
    total = added(3)
    for s in (0, 1):
        wait_bytes(o2f.at[s], o2_rf.at[s])
        total = total + o2f[s].astype(F32)
    out[...] = total.astype(BF16)

    wait_bytes(act.at[pl.ds(0, 31 * ROWS), :], act_ss)
    for k, (c0, cw) in enumerate(CHUNKS):
        wait_bytes(wbuf.at[pl.ds(0, 31 * ROWS), pl.ds(c0, cw)], w_ss.at[k])
    wait_bytes(dbuf.at[pl.ds(0, 31 * ROWS), :], d_ss)
    wait_bytes(part.at[pl.ds(0, 3 * QUARTER), :], r_ss)
    wait_bytes(xr, x_ss)
    wait_bytes(hid.at[pl.ds(0, 6 * BLOCK), :], h_ss)
    wait_bytes(ob.at[pl.ds(0, 3)], o1_ss)
    wait_bytes(o2s, o2_ss)


def per_device(activ, policy_gate, policy_up, policy_down, old_gate, old_up, old_down):
    sem = pltpu.SemaphoreType.DMA
    n = len(CHUNKS)
    return pl.pallas_call(
        kernel,
        name="layer",
        out_shape=pltpu.VMEM((BLOCK, FEATS), BF16),
        in_specs=[pl.BlockSpec(memory_space=pl.ANY)] * 7,
        out_specs=pl.BlockSpec(memory_space=pltpu.VMEM),
        scratch_shapes=[
            pltpu.VMEM((3, ROWS, CHIPS * UNITS), BF16),
            pltpu.VMEM((3, ROWS, CHIPS * UNITS), BF16),
            pltpu.VMEM((TOKENS, PLANE), BF16),
            pltpu.VMEM((PLANE, UNITS), BF16),
            pltpu.VMEM((PLANE, UNITS), BF16),
            pltpu.VMEM((TOKENS, UNITS), BF16),
            pltpu.VMEM((2, HALF, UNITS), BF16),
            pltpu.VMEM((2, QUARTER, UNITS), BF16),
            pltpu.VMEM((QUARTER, UNITS), F32),
            pltpu.VMEM((2 * BLOCK, UNITS), F32),
            pltpu.VMEM((8 * BLOCK, UNITS), BF16),
            pltpu.VMEM((SIDE, SIDE, BLOCK, FEATS), BF16),
            pltpu.VMEM((SIDE, 2, ROWS, FEATS), BF16),
            pltpu.VMEM((SIDE, 2, BLOCK, FEATS), BF16),
            pltpu.VMEM((3, BLOCK, FEATS), BF16),
            pltpu.VMEM((2, ROWS, FEATS), BF16),
            pltpu.VMEM((2, BLOCK, FEATS), BF16),
            pltpu.SemaphoreType.REGULAR((2,)),
            sem((7,)),
            sem, sem((CHIPS,)), sem,
            sem((n,)), sem((n,)),
            sem, sem((CHIPS,)), sem,
            sem, sem((n, 2)), sem((n, 2)),
            sem, sem((n,)),
            sem, sem((n, 2)), sem((n,)),
            sem, sem((SIDE, 2)), sem((SIDE, 2)),
            sem, sem((2,)), sem((2,)),
        ],
        compiler_params=pltpu.CompilerParams(
            collective_id=0, has_side_effects=True, vmem_limit_bytes=60 << 20
        ),
    )(activ, policy_gate, policy_up, policy_down.T, old_gate, old_up, old_down.T)


def solution(mesh):
    in_specs = (
        P("tp", "fsdp"),
        P(("fsdp", "tp"), None),
        P(("fsdp", "tp"), None),
        P(None, ("fsdp", "tp")),
        P(("fsdp", "tp"), None),
        P(("fsdp", "tp"), None),
        P(None, ("fsdp", "tp")),
    )
    return jax.shard_map(
        per_device, mesh=mesh, in_specs=in_specs, out_specs=P("tp", "fsdp"), check_vma=False
    )
```

```python
import functools

import jax
import jax.numpy as jnp
from jax import lax
from jax.experimental import pallas as pl
from jax.experimental.pallas import tpu as pltpu
from jax.sharding import PartitionSpec as P

MESH = pl.DeviceIdType.MESH
F32, BF16 = jnp.float32, jnp.bfloat16

SIDE = 4
CHIPS = 16
ROWS = 64
UNITS = 896
PLANE = 2048
TOKENS = 2048
QUARTER = 512
HALF = 256
BLOCK = 128
FEATS = 1024
CHUNKS = ((0, 128), (128, 128), (256, 128), (384, 128), (512, 128), (640, 128), (768, 128))

DOWN_PARTS = ((1, 8), (8, 16))


def device(x, y, z, c):
    return (y * 2 + x % 2, z * 4 + (x // 2) * 2 + c)


def shift(v, d):
    return lax.rem(v + d, SIDE)


def wait_bytes(ref, sem):
    pltpu.make_async_copy(ref, ref, sem).wait()


def mixed(a, b):
    return (0.6 * a.astype(F32) + 0.4 * b.astype(F32)).astype(BF16)


def kernel(
    act_in, pg_in, pu_in, pd_in, og_in, ou_in, od_in, out,
    mix, old, act, wbuf, dbuf, part, rl, rf, xs, xr, hid, ob, o1l, o1f, o2s, o2l, o2f,
    known, ld, act_ss, act_rs, act_fs, w_ss, w_rs, d_ss, d_rs, d_fs,
    r_ss, r_rl, r_rf, x_ss, x_rs, h_ss, h_rs, h_ro, o1_ss, o1_rl, o1_rf, o2_ss, o2_rl, o2_rf,
):
    f, t = lax.axis_index("fsdp"), lax.axis_index("tp")
    y, x_lo = f // 2, lax.rem(f, 2)
    z, x_hi, c = t // 4, lax.rem(t // 2, 2), lax.rem(t, 2)
    x = x_hi * 2 + x_lo
    first = c == 0
    chip = z * SIDE + x
    sibling = device(x, y, z, 1 - c)

    def send(src, dst, send_sem, recv_sem, to):
        pltpu.make_async_remote_copy(
            src_ref=src, dst_ref=dst, send_sem=send_sem, recv_sem=recv_sem, device_id=to, device_id_type=MESH
        ).start()

    def act_block(xx, zz, cc):
        tok = (zz * 4 + (xx // 2) * 2 + cc) * BLOCK
        return act.at[pl.ds(pl.multiple_of(tok, BLOCK), BLOCK), pl.ds(pl.multiple_of(lax.rem(xx, 2) * FEATS, FEATS), FEATS)]

    def weight_rows(xx, zz, cc):
        row = lax.rem(xx, 2) * FEATS + (zz * 2 + xx // 2) * 128 + cc * ROWS
        return pl.ds(pl.multiple_of(row, ROWS), ROWS)

    loads = [
        pltpu.make_async_copy(a, b, ld.at[i])
        for i, (a, b) in enumerate(
            [
                (act_in, act_block(x, z, c)),
                (pg_in, mix.at[0]), (og_in, old.at[0]),
                (pu_in, mix.at[1]), (ou_in, old.at[1]),
                (pd_in, mix.at[2]), (od_in, old.at[2]),
            ]
        )
    ]
    for copy in loads:
        copy.start()

    barrier = pltpu.get_barrier_semaphore()
    ring_x = [device(shift(x, d), y, z, c) for d in (1, 2, 3)]
    ring_z = [device(x, y, shift(z, d), c) for d in (1, 2, 3)]
    next_y = [device(x, shift(y, d), z, c) for d in (1, 3)]
    for to in (*ring_x, *ring_z, *next_y, sibling):
        pl.semaphore_signal(barrier, inc=1, device_id=to, device_id_type=MESH)
    pl.semaphore_wait(barrier, 9)

    def along_a(d):
        return jnp.where(first, shift(x, d), x), jnp.where(first, z, shift(z, d))

    def along_b(d):
        return jnp.where(first, x, shift(x, d)), jnp.where(first, shift(z, d), z)

    def block_of(da, db):
        return jnp.where(first, shift(x, da), shift(x, db)), jnp.where(first, shift(z, db), shift(z, da))

    def send_block(xx, zz, to, half=None):
        ref = act_block(xx, zz, c)
        if half is not None:
            ref = ref.at[pl.ds(half * ROWS, ROWS), :]
        send(ref, ref, act_ss, act_rs.at[zz * SIDE + xx], device(to[0], y, to[1], c))

    def share_block(xx, zz):
        ref = act_block(xx, zz, c)
        send(ref, ref, act_ss, act_fs, sibling)

    def await_block(da, db):
        xx, zz = block_of(da, db)
        wait_bytes(act_block(xx, zz, c), act_rs.at[zz * SIDE + xx])
        return xx, zz

    loads[0].wait()
    for d in (1, 3):
        send_block(x, z, along_a(d))
        send_block(x, z, along_b(d))
    share_block(x, z)

    for to in ring_z:
        pl.semaphore_signal(known.at[0], inc=1, device_id=to, device_id_type=MESH)
    pl.semaphore_wait(known.at[0], 3)
    pl.semaphore_signal(known.at[1], inc=1, device_id=sibling, device_id_type=MESH)
    pl.semaphore_wait(known.at[1], 1)

    def around(i):
        u, v = lax.rem(i, SIDE), lax.rem(i // SIDE + i, SIDE)
        return shift(x, jnp.where(first, u, v)), shift(z, jnp.where(first, v, u))

    def columns(p, c0, cw):
        return pl.ds(pl.multiple_of(p * UNITS + c0, 128), cw)

    def blend(m, p, c0, cw):
        cols = columns(p, c0, cw)
        mix[m, :, cols] = mixed(mix[m, :, cols], old[m, :, cols])

    def send_weights(k, then=None):
        c0, cw = CHUNKS[k]
        target = wbuf.at[weight_rows(x, z, c), pl.ds(c0, cw)]
        if then:
            then(chip)
        own = columns(chip, c0, cw)
        pltpu.make_async_copy(mix.at[c, :, own], target, w_rs.at[k]).start()
        send(mix.at[1 - c, :, own], target, w_ss.at[k], w_rs.at[k], sibling)

        def one(i, carry):
            xx, zz = around(i)
            p = zz * SIDE + xx
            if then:
                then(p)
            for m in (0, 1):
                send(mix.at[m, :, columns(p, c0, cw)], target, w_ss.at[k], w_rs.at[k], device(xx, y, zz, m))
            return carry

        lax.fori_loop(1, CHIPS, one, 0)

    def blend_first(p):
        for m in (0, 1):
            blend(m, p, *CHUNKS[0])

    def blend_rest(p, carry):
        for m in (0, 1):
            blend(m, p, CHUNKS[0][1], UNITS - CHUNKS[0][1])
        return carry

    def blend_down(p, carry):
        blend(2, p, 0, UNITS)
        return carry

    for copy in loads[1:5]:
        copy.wait()
    send_weights(0, blend_first)
    lax.fori_loop(0, CHIPS, blend_rest, 0)

    for s, da in ((0, 3), (1, 1), (None, 2)):
        xx, zz = await_block(da, 0)
        if s is not None:
            send_block(xx, zz, along_a((1, 3)[s]), s)
        for d in (1, 3):
            send_block(xx, zz, along_b(d))
        share_block(xx, zz)
    for da in (0, 3, 1, 2):
        for s, db in ((0, 3), (1, 1)):
            xx, zz = await_block(da, db)
            send_block(xx, zz, along_b((1, 3)[s]), s)
            share_block(xx, zz)

    send_weights(1)
    send_weights(2)

    for copy in loads[5:]:
        copy.wait()
    lax.fori_loop(0, CHIPS, blend_down, 0)

    def send_down(part):
        target = dbuf.at[weight_rows(x, z, c), :]
        if part == 0:
            pltpu.make_async_copy(mix.at[2, :, columns(chip, 0, UNITS)], target, d_rs.at[chip]).start()

        def one(i, carry):
            xx, zz = around(i)
            send(mix.at[2, :, columns(zz * SIDE + xx, 0, UNITS)], target, d_ss, d_rs.at[chip], device(xx, y, zz, c))
            return carry

        lax.fori_loop(*DOWN_PARTS[part], one, 0)

    def share_down():
        def one(i, carry):
            xx, zz = around(i)
            ref = dbuf.at[weight_rows(xx, zz, c), :]
            wait_bytes(ref, d_rs.at[zz * SIDE + xx])
            send(ref, ref, d_ss, d_fs, sibling)
            return carry

        lax.fori_loop(0, CHIPS, one, 0)

    for da in (0, 3, 1, 2):
        share_block(*await_block(da, 2))
    wait_bytes(act.at[pl.ds(0, TOKENS // 2), :], act_fs)

    def half_of(q, s):
        return pl.ds(pl.multiple_of(q * QUARTER + s * HALF, HALF), HALF)

    def multiply(k, *then):
        c0, cw = CHUNKS[k]
        cols = pl.ds(c0, cw)
        wait_bytes(wbuf.at[:, cols], w_rs.at[k])

        def one(i, carry):
            q = shift(y, jnp.where(i == 0, 2, jnp.where(i == 3, 0, 2 * i - 1)))
            rows = pl.ds(pl.multiple_of(q * QUARTER, QUARTER), QUARTER)
            part[rows, cols] = jnp.dot(act[rows, :], wbuf[:, cols], preferred_element_type=F32).astype(BF16)

            @pl.when(i == 0)
            def _():
                for s, d in ((0, 1), (1, 3)):
                    send(part.at[half_of(q, s), cols], rl.at[s, :, cols], r_ss, r_rl.at[k, s], device(x, shift(y, d), z, c))

            for s in (0, 1):

                @pl.when(i == s + 1)
                def _():
                    o = 1 - s
                    send(part.at[half_of(q, o), cols], rf.at[s, pl.ds(o * HALF, HALF), cols], r_ss, r_rf.at[k, s], device(x, q, z, c))

            return carry

        lax.fori_loop(0, 1, one, 0)
        for step, n in then:
            step(n)
        lax.fori_loop(1, SIDE, one, 0)

    def relay(k):
        c0, cw = CHUNKS[k]
        cols = pl.ds(c0, cw)
        for s, d in ((0, 1), (1, 3)):
            q = shift(y, d)
            rows = half_of(q, s)
            wait_bytes(rl.at[s, :, cols], r_rl.at[k, s])
            part[rows, cols] = (part[rows, cols].astype(F32) + rl[s, :, cols].astype(F32)).astype(BF16)
            send(part.at[rows, cols], rf.at[s, pl.ds(s * HALF, HALF), cols], r_ss, r_rf.at[k, s], device(x, q, z, c))

    def reduce(k):
        c0, cw = CHUNKS[k]
        cols = pl.ds(c0, cw)
        for s in (0, 1):
            wait_bytes(rf.at[s, :, cols], r_rf.at[k, s])

        def one(j, carry):
            rows = pl.ds(pl.multiple_of(j * BLOCK, BLOCK), BLOCK)
            total = part[pl.ds(pl.multiple_of(y * QUARTER + j * BLOCK, BLOCK), BLOCK), cols].astype(F32)
            xs[rows, cols] = total + rf[0, rows, cols].astype(F32) + rf[1, rows, cols].astype(F32)
            return carry

        lax.fori_loop(0, SIDE, one, 0)
        for j in (0, 1):
            rows = pl.ds(pl.multiple_of((2 * j + 1 - c) * BLOCK, BLOCK), BLOCK)
            send(xs.at[rows, cols], xr.at[pl.ds(j * BLOCK, BLOCK), cols], x_ss, x_rs.at[k], sibling)

    def activate(k):
        c0, cw = CHUNKS[k]
        cols = pl.ds(c0, cw)
        wait_bytes(xr.at[:, cols], x_rs.at[k])
        for j in (0, 1):
            own = xs[pl.ds(pl.multiple_of((2 * j + c) * BLOCK, BLOCK), BLOCK), cols]
            other = xr[pl.ds(j * BLOCK, BLOCK), cols]
            gate, up = jnp.where(first, own, other), jnp.where(first, other, own)
            hid[pl.ds(pl.multiple_of((y * 2 + j) * BLOCK, BLOCK), BLOCK), cols] = (jax.nn.silu(gate) * up).astype(BF16)
        ref = hid.at[pl.ds(pl.multiple_of(y * HALF, HALF), HALF), cols]
        for s, d in ((0, 1), (1, 3)):
            send(ref, ref, h_ss, h_rs.at[k, s], device(x, shift(y, d), z, c))

    def forward(k):
        c0, cw = CHUNKS[k]
        cols = pl.ds(c0, cw)
        for s, d in ((0, 1), (1, 3)):
            q = shift(y, SIDE - d)
            wait_bytes(hid.at[pl.ds(pl.multiple_of(q * HALF, HALF), HALF), cols], h_rs.at[k, s])
            ref = hid.at[pl.ds(pl.multiple_of(q * HALF + s * BLOCK, BLOCK), BLOCK), cols]
            send(ref, ref, h_ss, h_ro.at[k], device(x, shift(y, d), z, c))

    multiply(0, (send_weights, 3))
    multiply(1, (send_weights, 4))
    relay(0)
    multiply(2, (send_weights, 5))
    relay(1)
    reduce(0)
    multiply(3, (send_weights, 6))
    relay(2)
    reduce(1)
    activate(0)
    multiply(4)
    relay(3)
    reduce(2)
    activate(1)
    forward(0)
    multiply(5, (send_down, 0), (send_down, 1))
    relay(4)
    reduce(3)
    activate(2)
    forward(1)
    multiply(6)
    relay(5)
    reduce(4)
    activate(3)
    forward(2)
    relay(6)
    reduce(5)
    activate(4)
    forward(3)
    reduce(6)
    activate(5)
    forward(4)
    activate(6)
    forward(5)
    forward(6)
    share_down()
    wait_bytes(dbuf.at[pl.ds(0, PLANE // 2), :], d_fs)
    for k, (c0, cw) in enumerate(CHUNKS):
        wait_bytes(hid.at[pl.ds(0, HALF), pl.ds(c0, cw)], h_ro.at[k])

    a, b = jnp.where(first, z, x), jnp.where(first, x, z)
    first_to = [device(along_b(d)[0], y, along_b(d)[1], c) for d in (1, 3)]
    second_to = [device(along_a(d)[0], y, along_a(d)[1], c) for d in (1, 3)]
    ends = pl.ds(0, ROWS), pl.ds(ROWS, ROWS)

    def product(rows, n, width):
        tile = dbuf[pl.ds(pl.multiple_of(n * width, width), width), :]
        return lax.dot_general(rows, tile, (((1,), (1,)), ((), ())), preferred_element_type=F32).astype(BF16)

    def project(j):
        to = shift(b, (2, 1, 3, 0)[j])

        @pl.when(first)
        def _():
            rows = jnp.concatenate(
                [hid[pl.ds(pl.multiple_of((i * 2 + to // 2) * BLOCK, BLOCK), BLOCK), :] for i in range(SIDE)], axis=0
            )

            def one(n, carry):
                made = product(rows, lax.rem(to, 2) * 2 + n, 512)
                for i in range(SIDE):
                    ob[j, i, :, pl.ds(pl.multiple_of(n * 512, 512), 512)] = made[i * BLOCK : (i + 1) * BLOCK]
                return carry

            lax.fori_loop(0, 2, one, 0)

        @pl.when(c == 1)
        def _():
            def one(n, carry):
                made = product(hid[pl.ds(pl.multiple_of(to * HALF, HALF), HALF), :], n, FEATS)
                for h in (0, 1):
                    ob[j, h * 2 + n] = made[h * BLOCK : (h + 1) * BLOCK]
                return carry

            lax.fori_loop(0, 2, one, 0)

    def emit(j):
        for s, d in ((0, 1), (1, 3)):
            send(ob.at[j, shift(a, 2), ends[s]], o1l.at[j, s], o1_ss, o1_rl.at[j, s], first_to[s])
        for s, d in ((0, 1), (1, 3)):
            send(ob.at[j, shift(a, d), ends[1 - s]], o1f.at[j, s, ends[1 - s]], o1_ss, o1_rf.at[j, s], first_to[s])

    def pass_on(j):
        for s, d in ((0, 1), (1, 3)):
            i = shift(a, d)
            wait_bytes(o1l.at[j, s], o1_rl.at[j, s])
            ob[j, i, ends[s]] = (ob[j, i, ends[s]].astype(F32) + o1l[j, s].astype(F32)).astype(BF16)
            send(ob.at[j, i, ends[s]], o1f.at[j, s, ends[s]], o1_ss, o1_rf.at[j, s], first_to[s])

    def added(j):
        for s in (0, 1):
            wait_bytes(o1f.at[j, s], o1_rf.at[j, s])
        return ob[j, a].astype(F32) + o1f[j, 0].astype(F32) + o1f[j, 1].astype(F32)

    def finish(j):
        o2s[j] = added(j).astype(BF16)
        if j == 0:
            for s in (0, 1):
                send(o2s.at[0, ends[s]], o2l.at[s], o2_ss, o2_rl.at[s], second_to[s])
        else:
            s = j - 1
            send(o2s.at[j, ends[1 - s]], o2f.at[s, ends[1 - s]], o2_ss, o2_rf.at[s], second_to[s])

    def finish_far():
        for s in (0, 1):
            wait_bytes(o2l.at[s], o2_rl.at[s])
            o2s[s + 1, ends[s]] = (o2s[s + 1, ends[s]].astype(F32) + o2l[s].astype(F32)).astype(BF16)
            send(o2s.at[s + 1, ends[s]], o2f.at[s, ends[s]], o2_ss, o2_rf.at[s], second_to[s])

    project(0)
    emit(0)
    project(1)
    emit(1)
    project(2)
    emit(2)
    project(3)
    pass_on(0)
    pass_on(1)
    pass_on(2)
    emit(3)
    finish(0)
    finish(1)
    finish(2)
    pass_on(3)
    finish_far()
    total = added(3)
    for s in (0, 1):
        wait_bytes(o2f.at[s], o2_rf.at[s])
        total = total + o2f[s].astype(F32)
    out[...] = total.astype(BF16)

    wait_bytes(act.at[pl.ds(0, 31 * ROWS), :], act_ss)
    for k, (c0, cw) in enumerate(CHUNKS):
        wait_bytes(wbuf.at[pl.ds(0, 31 * ROWS), pl.ds(c0, cw)], w_ss.at[k])
    wait_bytes(dbuf.at[pl.ds(0, 31 * ROWS), :], d_ss)
    wait_bytes(part.at[pl.ds(0, 3 * QUARTER), :], r_ss)
    wait_bytes(xr, x_ss)
    wait_bytes(hid.at[pl.ds(0, 6 * BLOCK), :], h_ss)
    wait_bytes(ob.at[pl.ds(0, 3)], o1_ss)
    wait_bytes(o2s, o2_ss)


def per_device(activ, policy_gate, policy_up, policy_down, old_gate, old_up, old_down):
    sem = pltpu.SemaphoreType.DMA
    n = len(CHUNKS)
    return pl.pallas_call(
        kernel,
        name="layer",
        out_shape=pltpu.VMEM((BLOCK, FEATS), BF16),
        in_specs=[pl.BlockSpec(memory_space=pl.ANY)] * 7,
        out_specs=pl.BlockSpec(memory_space=pltpu.VMEM),
        scratch_shapes=[
            pltpu.VMEM((3, ROWS, CHIPS * UNITS), BF16),
            pltpu.VMEM((3, ROWS, CHIPS * UNITS), BF16),
            pltpu.VMEM((TOKENS, PLANE), BF16),
            pltpu.VMEM((PLANE, UNITS), BF16),
            pltpu.VMEM((PLANE, UNITS), BF16),
            pltpu.VMEM((TOKENS, UNITS), BF16),
            pltpu.VMEM((2, HALF, UNITS), BF16),
            pltpu.VMEM((2, QUARTER, UNITS), BF16),
            pltpu.VMEM((QUARTER, UNITS), F32),
            pltpu.VMEM((2 * BLOCK, UNITS), F32),
            pltpu.VMEM((8 * BLOCK, UNITS), BF16),
            pltpu.VMEM((SIDE, SIDE, BLOCK, FEATS), BF16),
            pltpu.VMEM((SIDE, 2, ROWS, FEATS), BF16),
            pltpu.VMEM((SIDE, 2, BLOCK, FEATS), BF16),
            pltpu.VMEM((3, BLOCK, FEATS), BF16),
            pltpu.VMEM((2, ROWS, FEATS), BF16),
            pltpu.VMEM((2, BLOCK, FEATS), BF16),
            pltpu.SemaphoreType.REGULAR((2,)),
            sem((7,)),
            sem, sem((CHIPS,)), sem,
            sem((n,)), sem((n,)),
            sem, sem((CHIPS,)), sem,
            sem, sem((n, 2)), sem((n, 2)),
            sem, sem((n,)),
            sem, sem((n, 2)), sem((n,)),
            sem, sem((SIDE, 2)), sem((SIDE, 2)),
            sem, sem((2,)), sem((2,)),
        ],
        compiler_params=pltpu.CompilerParams(
            collective_id=0, has_side_effects=True, vmem_limit_bytes=60 << 20
        ),
    )(activ, policy_gate, policy_up, policy_down.T, old_gate, old_up, old_down.T)


def solution(mesh):
    in_specs = (
        P("tp", "fsdp"),
        P(("fsdp", "tp"), None),
        P(("fsdp", "tp"), None),
        P(None, ("fsdp", "tp")),
        P(("fsdp", "tp"), None),
        P(("fsdp", "tp"), None),
        P(None, ("fsdp", "tp")),
    )
    return jax.shard_map(
        per_device, mesh=mesh, in_specs=in_specs, out_specs=P("tp", "fsdp"), check_vma=False
    )
```

```python
import functools

import jax
import jax.numpy as jnp
from jax import lax
from jax.experimental import pallas as pl
from jax.experimental.pallas import tpu as pltpu
from jax.sharding import PartitionSpec as P

MESH = pl.DeviceIdType.MESH
F32, BF16 = jnp.float32, jnp.bfloat16

SIDE = 4
CHIPS = 16
ROWS = 64
UNITS = 896
PLANE = 2048
TOKENS = 2048
QUARTER = 512
HALF = 256
BLOCK = 128
FEATS = 1024
CHUNKS = ((0, 128), (128, 128), (256, 128), (384, 128), (512, 128), (640, 128), (768, 128))

DOWN_PARTS = ((1, 8), (8, 16))


def device(x, y, z, c):
    return (y * 2 + x % 2, z * 4 + (x // 2) * 2 + c)


def shift(v, d):
    return lax.rem(v + d, SIDE)


def wait_bytes(ref, sem):
    pltpu.make_async_copy(ref, ref, sem).wait()


def mixed(a, b):
    return (0.6 * a.astype(F32) + 0.4 * b.astype(F32)).astype(BF16)


def kernel(
    act_in, pg_in, pu_in, pd_in, og_in, ou_in, od_in, out,
    mix, old, act, wbuf, dbuf, part, rl, rf, xs, xr, hid, ob, o1l, o1f, o2s, o2l, o2f,
    known, ld, act_ss, act_rs, act_fs, w_ss, w_rs, d_ss, d_rs, d_fs,
    r_ss, r_rl, r_rf, x_ss, x_rs, h_ss, h_rs, h_ro, o1_ss, o1_rl, o1_rf, o2_ss, o2_rl, o2_rf,
):
    f, t = lax.axis_index("fsdp"), lax.axis_index("tp")
    y, x_lo = f // 2, lax.rem(f, 2)
    z, x_hi, c = t // 4, lax.rem(t // 2, 2), lax.rem(t, 2)
    x = x_hi * 2 + x_lo
    first = c == 0
    chip = z * SIDE + x
    sibling = device(x, y, z, 1 - c)

    def send(src, dst, send_sem, recv_sem, to):
        pltpu.make_async_remote_copy(
            src_ref=src, dst_ref=dst, send_sem=send_sem, recv_sem=recv_sem, device_id=to, device_id_type=MESH
        ).start()

    def act_block(xx, zz, cc):
        tok = (zz * 4 + (xx // 2) * 2 + cc) * BLOCK
        return act.at[pl.ds(pl.multiple_of(tok, BLOCK), BLOCK), pl.ds(pl.multiple_of(lax.rem(xx, 2) * FEATS, FEATS), FEATS)]

    def weight_rows(xx, zz, cc):
        row = lax.rem(xx, 2) * FEATS + (zz * 2 + xx // 2) * 128 + cc * ROWS
        return pl.ds(pl.multiple_of(row, ROWS), ROWS)

    loads = [
        pltpu.make_async_copy(a, b, ld.at[i])
        for i, (a, b) in enumerate(
            [
                (act_in, act_block(x, z, c)),
                (pg_in, mix.at[0]), (og_in, old.at[0]),
                (pu_in, mix.at[1]), (ou_in, old.at[1]),
                (pd_in, mix.at[2]), (od_in, old.at[2]),
            ]
        )
    ]
    for copy in loads:
        copy.start()

    barrier = pltpu.get_barrier_semaphore()
    ring_x = [device(shift(x, d), y, z, c) for d in (1, 2, 3)]
    ring_z = [device(x, y, shift(z, d), c) for d in (1, 2, 3)]
    next_y = [device(x, shift(y, d), z, c) for d in (1, 3)]
    for to in (*ring_x, *ring_z, *next_y, sibling):
        pl.semaphore_signal(barrier, inc=1, device_id=to, device_id_type=MESH)
    pl.semaphore_wait(barrier, 9)

    def along_a(d):
        return jnp.where(first, shift(x, d), x), jnp.where(first, z, shift(z, d))

    def along_b(d):
        return jnp.where(first, x, shift(x, d)), jnp.where(first, shift(z, d), z)

    def block_of(da, db):
        return jnp.where(first, shift(x, da), shift(x, db)), jnp.where(first, shift(z, db), shift(z, da))

    def send_block(xx, zz, to, half=None):
        ref = act_block(xx, zz, c)
        if half is not None:
            ref = ref.at[pl.ds(half * ROWS, ROWS), :]
        send(ref, ref, act_ss, act_rs.at[zz * SIDE + xx], device(to[0], y, to[1], c))

    def share_block(xx, zz):
        ref = act_block(xx, zz, c)
        send(ref, ref, act_ss, act_fs, sibling)

    def await_block(da, db):
        xx, zz = block_of(da, db)
        wait_bytes(act_block(xx, zz, c), act_rs.at[zz * SIDE + xx])
        return xx, zz

    loads[0].wait()
    for d in (1, 3):
        send_block(x, z, along_a(d))
        send_block(x, z, along_b(d))
    share_block(x, z)

    for to in ring_z:
        pl.semaphore_signal(known.at[0], inc=1, device_id=to, device_id_type=MESH)
    pl.semaphore_wait(known.at[0], 3)
    pl.semaphore_signal(known.at[1], inc=1, device_id=sibling, device_id_type=MESH)
    pl.semaphore_wait(known.at[1], 1)

    def around(i):
        u, v = lax.rem(i, SIDE), lax.rem(i // SIDE + i, SIDE)
        return shift(x, jnp.where(first, u, v)), shift(z, jnp.where(first, v, u))

    def columns(p, c0, cw):
        return pl.ds(pl.multiple_of(p * UNITS + c0, 128), cw)

    def blend(m, p, c0, cw):
        cols = columns(p, c0, cw)
        mix[m, :, cols] = mixed(mix[m, :, cols], old[m, :, cols])

    def send_weights(k, then=None):
        c0, cw = CHUNKS[k]
        target = wbuf.at[weight_rows(x, z, c), pl.ds(c0, cw)]
        if then:
            then(chip)
        own = columns(chip, c0, cw)
        pltpu.make_async_copy(mix.at[c, :, own], target, w_rs.at[k]).start()
        send(mix.at[1 - c, :, own], target, w_ss.at[k], w_rs.at[k], sibling)

        def one(i, carry):
            xx, zz = around(i)
            p = zz * SIDE + xx
            if then:
                then(p)
            for m in (0, 1):
                send(mix.at[m, :, columns(p, c0, cw)], target, w_ss.at[k], w_rs.at[k], device(xx, y, zz, m))
            return carry

        lax.fori_loop(1, CHIPS, one, 0)

    def blend_first(p):
        for m in (0, 1):
            blend(m, p, *CHUNKS[0])

    def blend_rest(p, carry):
        for m in (0, 1):
            blend(m, p, CHUNKS[0][1], UNITS - CHUNKS[0][1])
        return carry

    def blend_down(p, carry):
        blend(2, p, 0, UNITS)
        return carry

    for copy in loads[1:5]:
        copy.wait()
    send_weights(0, blend_first)
    lax.fori_loop(0, CHIPS, blend_rest, 0)

    for s, da in ((0, 3), (1, 1), (None, 2)):
        xx, zz = await_block(da, 0)
        if s is not None:
            send_block(xx, zz, along_a((1, 3)[s]), s)
        for d in (1, 3):
            send_block(xx, zz, along_b(d))
        share_block(xx, zz)
    for da in (0, 3, 1, 2):
        for s, db in ((0, 3), (1, 1)):
            xx, zz = await_block(da, db)
            send_block(xx, zz, along_b((1, 3)[s]), s)
            share_block(xx, zz)

    send_weights(1)
    send_weights(2)

    for copy in loads[5:]:
        copy.wait()
    lax.fori_loop(0, CHIPS, blend_down, 0)

    def send_down(part):
        target = dbuf.at[weight_rows(x, z, c), :]
        if part == 0:
            pltpu.make_async_copy(mix.at[2, :, columns(chip, 0, UNITS)], target, d_rs.at[chip]).start()

        def one(i, carry):
            xx, zz = around(i)
            send(mix.at[2, :, columns(zz * SIDE + xx, 0, UNITS)], target, d_ss, d_rs.at[chip], device(xx, y, zz, c))
            return carry

        lax.fori_loop(*DOWN_PARTS[part], one, 0)

    def share_down():
        def one(i, carry):
            xx, zz = around(i)
            ref = dbuf.at[weight_rows(xx, zz, c), :]
            wait_bytes(ref, d_rs.at[zz * SIDE + xx])
            send(ref, ref, d_ss, d_fs, sibling)
            return carry

        lax.fori_loop(0, CHIPS, one, 0)

    for da in (0, 3, 1, 2):
        share_block(*await_block(da, 2))
    wait_bytes(act.at[pl.ds(0, TOKENS // 2), :], act_fs)

    def half_of(q, s):
        return pl.ds(pl.multiple_of(q * QUARTER + s * HALF, HALF), HALF)

    def multiply(k, *then):
        c0, cw = CHUNKS[k]
        cols = pl.ds(c0, cw)
        wait_bytes(wbuf.at[:, cols], w_rs.at[k])

        def one(i, carry):
            q = shift(y, jnp.where(i == 0, 2, jnp.where(i == 3, 0, 2 * i - 1)))
            rows = pl.ds(pl.multiple_of(q * QUARTER, QUARTER), QUARTER)
            part[rows, cols] = jnp.dot(act[rows, :], wbuf[:, cols], preferred_element_type=F32).astype(BF16)

            @pl.when(i == 0)
            def _():
                for s, d in ((0, 1), (1, 3)):
                    send(part.at[half_of(q, s), cols], rl.at[s, :, cols], r_ss, r_rl.at[k, s], device(x, shift(y, d), z, c))

            for s in (0, 1):

                @pl.when(i == s + 1)
                def _():
                    o = 1 - s
                    send(part.at[half_of(q, o), cols], rf.at[s, pl.ds(o * HALF, HALF), cols], r_ss, r_rf.at[k, s], device(x, q, z, c))

            return carry

        lax.fori_loop(0, 2, one, 0)
        for step, n in then:
            step(n)
        lax.fori_loop(2, SIDE, one, 0)

    def relay(k):
        c0, cw = CHUNKS[k]
        cols = pl.ds(c0, cw)
        for s, d in ((0, 1), (1, 3)):
            q = shift(y, d)
            rows = half_of(q, s)
            wait_bytes(rl.at[s, :, cols], r_rl.at[k, s])
            part[rows, cols] = (part[rows, cols].astype(F32) + rl[s, :, cols].astype(F32)).astype(BF16)
            send(part.at[rows, cols], rf.at[s, pl.ds(s * HALF, HALF), cols], r_ss, r_rf.at[k, s], device(x, q, z, c))

    def reduce(k):
        c0, cw = CHUNKS[k]
        cols = pl.ds(c0, cw)
        for s in (0, 1):
            wait_bytes(rf.at[s, :, cols], r_rf.at[k, s])

        def one(j, carry):
            rows = pl.ds(pl.multiple_of(j * BLOCK, BLOCK), BLOCK)
            total = part[pl.ds(pl.multiple_of(y * QUARTER + j * BLOCK, BLOCK), BLOCK), cols].astype(F32)
            xs[rows, cols] = total + rf[0, rows, cols].astype(F32) + rf[1, rows, cols].astype(F32)
            return carry

        lax.fori_loop(0, SIDE, one, 0)
        for j in (0, 1):
            rows = pl.ds(pl.multiple_of((2 * j + 1 - c) * BLOCK, BLOCK), BLOCK)
            send(xs.at[rows, cols], xr.at[pl.ds(j * BLOCK, BLOCK), cols], x_ss, x_rs.at[k], sibling)

    def activate(k):
        c0, cw = CHUNKS[k]
        cols = pl.ds(c0, cw)
        wait_bytes(xr.at[:, cols], x_rs.at[k])
        for j in (0, 1):
            own = xs[pl.ds(pl.multiple_of((2 * j + c) * BLOCK, BLOCK), BLOCK), cols]
            other = xr[pl.ds(j * BLOCK, BLOCK), cols]
            gate, up = jnp.where(first, own, other), jnp.where(first, other, own)
            hid[pl.ds(pl.multiple_of((y * 2 + j) * BLOCK, BLOCK), BLOCK), cols] = (jax.nn.silu(gate) * up).astype(BF16)
        ref = hid.at[pl.ds(pl.multiple_of(y * HALF, HALF), HALF), cols]
        for s, d in ((0, 1), (1, 3)):
            send(ref, ref, h_ss, h_rs.at[k, s], device(x, shift(y, d), z, c))

    def forward(k):
        c0, cw = CHUNKS[k]
        cols = pl.ds(c0, cw)
        for s, d in ((0, 1), (1, 3)):
            q = shift(y, SIDE - d)
            wait_bytes(hid.at[pl.ds(pl.multiple_of(q * HALF, HALF), HALF), cols], h_rs.at[k, s])
            ref = hid.at[pl.ds(pl.multiple_of(q * HALF + s * BLOCK, BLOCK), BLOCK), cols]
            send(ref, ref, h_ss, h_ro.at[k], device(x, shift(y, d), z, c))

    multiply(0, (send_weights, 3))
    multiply(1, (send_weights, 4))
    relay(0)
    multiply(2, (send_weights, 5))
    relay(1)
    reduce(0)
    multiply(3, (send_weights, 6))
    relay(2)
    reduce(1)
    activate(0)
    multiply(4)
    relay(3)
    reduce(2)
    activate(1)
    forward(0)
    multiply(5, (send_down, 0), (send_down, 1))
    relay(4)
    reduce(3)
    activate(2)
    forward(1)
    multiply(6)
    relay(5)
    reduce(4)
    activate(3)
    forward(2)
    relay(6)
    reduce(5)
    activate(4)
    forward(3)
    reduce(6)
    activate(5)
    forward(4)
    activate(6)
    forward(5)
    forward(6)
    share_down()
    wait_bytes(dbuf.at[pl.ds(0, PLANE // 2), :], d_fs)
    for k, (c0, cw) in enumerate(CHUNKS):
        wait_bytes(hid.at[pl.ds(0, HALF), pl.ds(c0, cw)], h_ro.at[k])

    a, b = jnp.where(first, z, x), jnp.where(first, x, z)
    first_to = [device(along_b(d)[0], y, along_b(d)[1], c) for d in (1, 3)]
    second_to = [device(along_a(d)[0], y, along_a(d)[1], c) for d in (1, 3)]
    ends = pl.ds(0, ROWS), pl.ds(ROWS, ROWS)

    def product(rows, n, width):
        tile = dbuf[pl.ds(pl.multiple_of(n * width, width), width), :]
        return lax.dot_general(rows, tile, (((1,), (1,)), ((), ())), preferred_element_type=F32).astype(BF16)

    def project(j):
        to = shift(b, (2, 1, 3, 0)[j])

        @pl.when(first)
        def _():
            rows = jnp.concatenate(
                [hid[pl.ds(pl.multiple_of((i * 2 + to // 2) * BLOCK, BLOCK), BLOCK), :] for i in range(SIDE)], axis=0
            )

            def one(n, carry):
                made = product(rows, lax.rem(to, 2) * 2 + n, 512)
                for i in range(SIDE):
                    ob[j, i, :, pl.ds(pl.multiple_of(n * 512, 512), 512)] = made[i * BLOCK : (i + 1) * BLOCK]
                return carry

            lax.fori_loop(0, 2, one, 0)

        @pl.when(c == 1)
        def _():
            def one(n, carry):
                made = product(hid[pl.ds(pl.multiple_of(to * HALF, HALF), HALF), :], n, FEATS)
                for h in (0, 1):
                    ob[j, h * 2 + n] = made[h * BLOCK : (h + 1) * BLOCK]
                return carry

            lax.fori_loop(0, 2, one, 0)

    def emit(j):
        for s, d in ((0, 1), (1, 3)):
            send(ob.at[j, shift(a, 2), ends[s]], o1l.at[j, s], o1_ss, o1_rl.at[j, s], first_to[s])
        for s, d in ((0, 1), (1, 3)):
            send(ob.at[j, shift(a, d), ends[1 - s]], o1f.at[j, s, ends[1 - s]], o1_ss, o1_rf.at[j, s], first_to[s])

    def pass_on(j):
        for s, d in ((0, 1), (1, 3)):
            i = shift(a, d)
            wait_bytes(o1l.at[j, s], o1_rl.at[j, s])
            ob[j, i, ends[s]] = (ob[j, i, ends[s]].astype(F32) + o1l[j, s].astype(F32)).astype(BF16)
            send(ob.at[j, i, ends[s]], o1f.at[j, s, ends[s]], o1_ss, o1_rf.at[j, s], first_to[s])

    def added(j):
        for s in (0, 1):
            wait_bytes(o1f.at[j, s], o1_rf.at[j, s])
        return ob[j, a].astype(F32) + o1f[j, 0].astype(F32) + o1f[j, 1].astype(F32)

    def finish(j):
        o2s[j] = added(j).astype(BF16)
        if j == 0:
            for s in (0, 1):
                send(o2s.at[0, ends[s]], o2l.at[s], o2_ss, o2_rl.at[s], second_to[s])
        else:
            s = j - 1
            send(o2s.at[j, ends[1 - s]], o2f.at[s, ends[1 - s]], o2_ss, o2_rf.at[s], second_to[s])

    def finish_far():
        for s in (0, 1):
            wait_bytes(o2l.at[s], o2_rl.at[s])
            o2s[s + 1, ends[s]] = (o2s[s + 1, ends[s]].astype(F32) + o2l[s].astype(F32)).astype(BF16)
            send(o2s.at[s + 1, ends[s]], o2f.at[s, ends[s]], o2_ss, o2_rf.at[s], second_to[s])

    project(0)
    emit(0)
    project(1)
    emit(1)
    project(2)
    emit(2)
    project(3)
    pass_on(0)
    pass_on(1)
    pass_on(2)
    emit(3)
    finish(0)
    finish(1)
    finish(2)
    pass_on(3)
    finish_far()
    total = added(3)
    for s in (0, 1):
        wait_bytes(o2f.at[s], o2_rf.at[s])
        total = total + o2f[s].astype(F32)
    out[...] = total.astype(BF16)

    wait_bytes(act.at[pl.ds(0, 31 * ROWS), :], act_ss)
    for k, (c0, cw) in enumerate(CHUNKS):
        wait_bytes(wbuf.at[pl.ds(0, 31 * ROWS), pl.ds(c0, cw)], w_ss.at[k])
    wait_bytes(dbuf.at[pl.ds(0, 31 * ROWS), :], d_ss)
    wait_bytes(part.at[pl.ds(0, 3 * QUARTER), :], r_ss)
    wait_bytes(xr, x_ss)
    wait_bytes(hid.at[pl.ds(0, 6 * BLOCK), :], h_ss)
    wait_bytes(ob.at[pl.ds(0, 3)], o1_ss)
    wait_bytes(o2s, o2_ss)


def per_device(activ, policy_gate, policy_up, policy_down, old_gate, old_up, old_down):
    sem = pltpu.SemaphoreType.DMA
    n = len(CHUNKS)
    return pl.pallas_call(
        kernel,
        name="layer",
        out_shape=pltpu.VMEM((BLOCK, FEATS), BF16),
        in_specs=[pl.BlockSpec(memory_space=pl.ANY)] * 7,
        out_specs=pl.BlockSpec(memory_space=pltpu.VMEM),
        scratch_shapes=[
            pltpu.VMEM((3, ROWS, CHIPS * UNITS), BF16),
            pltpu.VMEM((3, ROWS, CHIPS * UNITS), BF16),
            pltpu.VMEM((TOKENS, PLANE), BF16),
            pltpu.VMEM((PLANE, UNITS), BF16),
            pltpu.VMEM((PLANE, UNITS), BF16),
            pltpu.VMEM((TOKENS, UNITS), BF16),
            pltpu.VMEM((2, HALF, UNITS), BF16),
            pltpu.VMEM((2, QUARTER, UNITS), BF16),
            pltpu.VMEM((QUARTER, UNITS), F32),
            pltpu.VMEM((2 * BLOCK, UNITS), F32),
            pltpu.VMEM((8 * BLOCK, UNITS), BF16),
            pltpu.VMEM((SIDE, SIDE, BLOCK, FEATS), BF16),
            pltpu.VMEM((SIDE, 2, ROWS, FEATS), BF16),
            pltpu.VMEM((SIDE, 2, BLOCK, FEATS), BF16),
            pltpu.VMEM((3, BLOCK, FEATS), BF16),
            pltpu.VMEM((2, ROWS, FEATS), BF16),
            pltpu.VMEM((2, BLOCK, FEATS), BF16),
            pltpu.SemaphoreType.REGULAR((2,)),
            sem((7,)),
            sem, sem((CHIPS,)), sem,
            sem((n,)), sem((n,)),
            sem, sem((CHIPS,)), sem,
            sem, sem((n, 2)), sem((n, 2)),
            sem, sem((n,)),
            sem, sem((n, 2)), sem((n,)),
            sem, sem((SIDE, 2)), sem((SIDE, 2)),
            sem, sem((2,)), sem((2,)),
        ],
        compiler_params=pltpu.CompilerParams(
            collective_id=0, has_side_effects=True, vmem_limit_bytes=60 << 20
        ),
    )(activ, policy_gate, policy_up, policy_down.T, old_gate, old_up, old_down.T)


def solution(mesh):
    in_specs = (
        P("tp", "fsdp"),
        P(("fsdp", "tp"), None),
        P(("fsdp", "tp"), None),
        P(None, ("fsdp", "tp")),
        P(("fsdp", "tp"), None),
        P(("fsdp", "tp"), None),
        P(None, ("fsdp", "tp")),
    )
    return jax.shard_map(
        per_device, mesh=mesh, in_specs=in_specs, out_specs=P("tp", "fsdp"), check_vma=False
    )
```
